256 devices in a mesh: group: 2 (over core), dp: 16 (over y, x), mp: 8 (over z).
Axes of the slice: x: 4, y: 4, z: 8, core: 2. Of those that a mesh axis runs over, the one named last changes fastest.
Arguments:
- queries: bfloat16 [8192, 1024], P(('group', 'dp')), may hold values from -6 to 6
- clips: bfloat16 [65536, 1024], P(('group', 'dp')), may hold values from -6 to 6
- norm_gain: float32 [1024], replicated, may hold values from 0.1 to 1.9
- w_in: bfloat16 [1024, 2, 4096], P(None, None, 'mp'), may hold values from -0.1875 to 0.1875
- w_out: bfloat16 [4096, 1024], P('mp'), may hold values from -0.09375 to 0.09375
- proj: bfloat16 [1024, 768], replicated, may hold values from -0.1875 to 0.1875
- pos_row: int32 [8192], P(('group', 'dp', 'mp')), may hold values from 0 to 255
- neg_owner: int32 [8192, 8], P(('group', 'dp', 'mp')), may hold values from 0 to 127, all different within a row; in each aligned block of 32 rows (0 to 31, 32 to 63, ...) at most 8 rows name the same one
- neg_row: int32 [8192, 8], P(('group', 'dp', 'mp')), may hold values from 0 to 255
- clip_dest: int32 [65536, 1], P(('group', 'dp', 'mp')), may hold values from 0 to 31; in each aligned block of 256 rows (0 to 255, 256 to 511, ...) at most 16 rows name the same one
Outputs:
- losses: float32 [8192], P(('group', 'dp', 'mp'))
- index_shard: bfloat16 [131072, 768], P(('group', 'dp', 'mp'))
- grad_proj: float32 [1024, 768], P(('group', 'dp', 'mp'))
The draws below stay inside these ranges and needn't reach their ends.
Inputs may be any that keep to these rules, and one draw needn't show every extreme that they name: `neg_owner`: each query's 8 owners differ. In each aligned block of 32 rows (the rows of one device) at most 8 rows name one owner, and some block reaches 8. `clip_dest`: in each aligned block of 256 rows (the clips of one device) at most 16 name one owner, and some block reaches 16.
All inputs are finite; a program needn't handle non-finite values.
Results may differ from the reference program's by a relative error of at most 0.013.
Values may be sent and summed in bfloat16 or wider, within the bound.
A program may use at most 128 MiB of HBM per device.

```python
import math
import jax
import jax.numpy as jnp
import numpy as np
from jax import lax

D = 1024
FF = 4096
E = 768
K = 8
Q_DEV = 256
C_DEV = 2048
Q_LOC = 32
C_LOC = 256
CAPN = 8
CAPI = 16
QUERIES = 8192
CLIPS = 65536
INDEX_ROWS = 131072
N_GROUP = 2
N_DP = 16
N_MP = 8


def set_ends(drawn, stream_key, least, largest):
    place = [jax.random.randint(jax.random.fold_in(stream_key, axis), (), 0, length) for axis, length in enumerate(drawn.shape)]
    widest = drawn.shape.index(max(drawn.shape))
    beside = place[:widest] + [(place[widest] + 1) % drawn.shape[widest]] + place[widest + 1:]
    return drawn.at[tuple(place)].set(least).at[tuple(beside)].set(largest)


def levels(stream_key, extent, split, low, largest):
    def one(axis_at, parts):
        heights = jax.random.uniform(jax.random.fold_in(jax.random.fold_in(stream_key, 6), axis_at), (parts,), jnp.float32, low / len(split), largest / len(split))
        return jnp.repeat(jnp.exp(heights), extent[axis_at] // parts).reshape((-1,) + (1,) * (len(extent) - axis_at - 1))

    loudness = one(*split[0])
    for cut in split[1:]:
        loudness = loudness * one(*cut)
    return loudness


def assign_block(rng, own, number, rows, count, top, most, skew):
    sequence = jax.random.permutation(rng, count)
    heavy_load, usual = load_shares(count, rows * top, most, skew, True), load_shares(count, rows * top, most, skew, False)
    places = jnp.arange(count)

    def named(lengths, turn):
        used = int((lengths > 0).sum())
        fixed = max(1, used // 4)
        moved = fixed + (places - fixed + turn * (used - fixed)) % max(1, count - fixed)
        return jnp.zeros((count,), jnp.int32).at[sequence[jnp.where(places < fixed, places, moved)]].set(jnp.asarray(lengths, jnp.int32))

    lengths = jnp.where(number % 4 == 0, named(heavy_load, number // 4), named(usual, number - number // 4 - 1))
    mixed = jax.random.permutation(jax.random.fold_in(own, 3), count)
    giver, taker = mixed[0:count // 2 * 2:2], mixed[1:count // 2 * 2:2]
    margin = jnp.minimum(lengths[giver] - 1, most - lengths[taker]) // 2
    margin = jnp.where((giver == sequence[0]) | (taker == sequence[0]) | (lengths[taker] == 0), 0, jnp.maximum(margin, 0))
    moved = jax.random.randint(jax.random.fold_in(own, 4), (count // 2,), 0, 1 << 20) % (margin + 1)
    lengths = lengths.at[giver].add(-moved).at[taker].add(moved)
    labels = jnp.searchsorted(jnp.cumsum(lengths), jnp.arange(rows * top), side="right").astype(jnp.int32)
    grid = labels.reshape(top, rows).T
    grid = grid[jax.random.permutation(jax.random.fold_in(own, 1), rows)]
    turn = jax.random.randint(jax.random.fold_in(own, 2), (rows, 1), 0, top)
    return jnp.take_along_axis(grid, (jnp.arange(top)[None, :] + turn) % top, axis=1)


def load_shares(amount, total, most, slope, full):
    loads = [(1 << 20) // math.isqrt(grade ** slope) + 1 for grade in range(1, amount + 1)]
    largest = most if full else min(most, max(-(-total // amount), total * loads[0] // sum(loads)))
    least = 1 if total - largest >= amount - 1 else 0
    holding, surplus = [largest] + [least] * (amount - 1), total - largest - least * (amount - 1)
    while surplus > 0:
        free = [i for i in range(1, amount) if holding[i] < largest] or [i for i in range(1, amount) if holding[i] < most]
        pool, left = sum([loads[i] for i in free]), surplus
        for i in free:
            extra = min(most - holding[i], max(1, left * loads[i] // pool), surplus)
            holding[i] = holding[i] + extra
            surplus = surplus - extra
    return np.array(holding)


def centred(own_key, dims, width, limit, cuts=(), kind=jnp.bfloat16):
    array = jax.random.normal(own_key, dims, jnp.float32) * width
    if len(cuts) > 0:
        array = levels(own_key, dims, cuts, -0.22, 0.18) * array
    return jnp.clip(array, min=-limit, max=limit).astype(kind)


def setup_inputs(seed: int = 0) -> dict:
    key_list = jax.random.split(jax.random.key(seed), 11)
    queries = centred(key_list[0], (QUERIES, D), 1.0, 6.0, ((0, 32),))
    clips = centred(key_list[1], (CLIPS, D), 1.0, 6.0, ((0, 32),))
    norm_gain = jnp.clip(1.0 + 0.18 * jax.random.normal(key_list[2], (D,), jnp.float32), 0.1, 1.9)
    w_in = centred(key_list[3], (D, 2, FF), D ** -0.5, 0.1875, ((2, 8),))
    w_out = centred(key_list[4], (FF, D), FF ** -0.5, 0.09375, ((0, 8),))
    proj = centred(key_list[5], (D, E), D ** -0.5, 0.1875)
    pos_row = set_ends(jax.random.randint(key_list[6], (QUERIES,), 0, C_LOC), jax.random.fold_in(key_list[6], 1), 0, C_LOC - 1).astype(jnp.int32)
    neg_owner_keys = jax.random.split(jax.random.fold_in(key_list[7], 1), QUERIES // Q_LOC)
    neg_owner_turns = jax.random.permutation(jax.random.fold_in(key_list[7], 3), QUERIES // Q_LOC)
    neg_owner = jax.vmap(lambda own, number: assign_block(jax.random.fold_in(key_list[7], 2), own, number, Q_LOC, N_DP * N_MP, K, CAPN, 2))(neg_owner_keys, neg_owner_turns).reshape((QUERIES, K))
    neg_row = set_ends(jax.random.randint(key_list[8], (QUERIES, K), 0, C_LOC), jax.random.fold_in(key_list[8], 1), 0, C_LOC - 1).astype(jnp.int32)
    clip_dest_keys = jax.random.split(jax.random.fold_in(key_list[9], 1), CLIPS // C_LOC)
    clip_dest_turns = jax.random.permutation(jax.random.fold_in(key_list[9], 3), CLIPS // C_LOC)
    clip_dest = jax.vmap(lambda own, number: assign_block(jax.random.fold_in(key_list[9], 2), own, number, C_LOC, N_GROUP * N_DP, 1, CAPI, 1))(clip_dest_keys, clip_dest_turns).reshape((CLIPS, 1))
    return {"queries": queries, "clips": clips, "norm_gain": norm_gain, "w_in": w_in, "w_out": w_out, "proj": proj, "pos_row": pos_row, "neg_owner": neg_owner, "neg_row": neg_row, "clip_dest": clip_dest}


norm_eps = 1e-06
embed_eps = 1e-06
score_scale = 20.0

def encode(rows, norm_gain, w_in, w_out, proj):
    values = rows.astype(jnp.float32)
    scale = lax.rsqrt(lax.optimization_barrier(jnp.mean(values * values, axis=-1, keepdims=True)) + norm_eps)
    normed = (values * scale * norm_gain).astype(jnp.bfloat16)
    gate = jnp.dot(normed, w_in[:, 0, :], preferred_element_type=jnp.float32)
    upper = jnp.dot(normed, w_in[:, 1, :], preferred_element_type=jnp.float32)
    hidden = (jax.nn.silu(gate) * upper).astype(jnp.bfloat16)
    mixed = jnp.dot(hidden, w_out, preferred_element_type=jnp.float32)
    summed = (values + mixed).astype(jnp.bfloat16)
    raw = jnp.dot(summed, proj, preferred_element_type=jnp.float32)
    length = jnp.sqrt(lax.optimization_barrier(jnp.sum(raw * raw, axis=-1, keepdims=True)) + embed_eps)
    return (summed, length, raw / length)

def encode_all(rows, per_block, norm_gain, w_in, w_out, proj):
    blocks = rows.shape[0] // per_block

    def one_block(block_rows):
        return encode(block_rows, norm_gain, w_in, w_out, proj)
    summed, length, unit = lax.map(one_block, rows.reshape(blocks, per_block, rows.shape[1]))
    return (summed.reshape(-1, summed.shape[-1]), length.reshape(-1, 1), unit.reshape(-1, unit.shape[-1]))

def reference(queries, clips, norm_gain, w_in, w_out, proj, pos_row, neg_owner, neg_row, clip_dest):
    query_summed, query_length, query_unit = encode_all(queries, Q_DEV, norm_gain, w_in, w_out, proj)
    clip_summed, clip_length, clip_unit = encode_all(clips, C_DEV, norm_gain, w_in, w_out, proj)
    query_embed = query_unit.astype(jnp.bfloat16)
    clip_embed = clip_unit.astype(jnp.bfloat16)
    owners = N_GROUP * N_DP
    blocks = CLIPS // C_LOC
    destination = clip_dest[:, 0].reshape(blocks, C_LOC)
    onehot = (destination[:, :, None] == jnp.arange(owners, dtype=jnp.int32)[None, None, :]).astype(jnp.int32)
    slot = lax.optimization_barrier(jnp.sum(jnp.cumsum(onehot, axis=1) * onehot, axis=-1)) - 1
    block_ids = jnp.arange(blocks, dtype=jnp.int32)[:, None]
    mp_place = block_ids % N_MP
    source = block_ids // N_MP
    target = ((destination * N_MP + mp_place) * owners + source) * CAPI + slot
    index_shard = jnp.zeros((INDEX_ROWS, E), jnp.bfloat16).at[target.reshape(-1)].set(clip_embed)
    query_ids = jnp.arange(QUERIES, dtype=jnp.int32)
    home = query_ids // Q_LOC
    positive = home * C_LOC + pos_row
    base = home // (N_DP * N_MP) * (N_DP * N_MP)
    negative = (base[:, None] + neg_owner) * C_LOC + neg_row
    picks = jnp.concatenate([positive[:, None], negative], axis=1)
    candidates = clip_embed[picks].astype(jnp.float32)
    scores = score_scale * jnp.einsum('qe,qce->qc', query_embed.astype(jnp.float32), candidates)
    weights = jnp.exp(scores)
    total = lax.optimization_barrier(jnp.sum(weights, axis=-1))
    losses = jnp.log(total) - scores[:, 0]
    probs = weights / total[:, None]
    dunit = score_scale * (jnp.einsum('qc,qce->qe', probs, candidates) - candidates[:, 0, :])
    along = lax.optimization_barrier(jnp.sum(query_unit * dunit, axis=-1, keepdims=True))
    draw = ((dunit - query_unit * along) / query_length).astype(jnp.bfloat16)
    grad_proj = lax.dot_general(query_summed, draw, (((0,), (0,)), ((), ())), preferred_element_type=jnp.float32)
    return (losses, index_shard, grad_proj)
```

```python
import jax
import jax.numpy as jnp
from jax import lax
from jax.experimental import pallas as pl
from jax.experimental.pallas import tpu as pltpu
from jax.sharding import PartitionSpec as P

norm_eps = 1e-06
embed_eps = 1e-06
score_scale = 20.0
MESH = pl.DeviceIdType.MESH
f32 = jnp.float32
bf16 = jnp.bfloat16


def part_of(way, dist):
    return 0 if dist == 4 else 7 - 2 * dist + way


def encode_kernel(
    q_hbm, c_hbm, gain_ref, win_hbm, wout_hbm, proj_hbm,
    embc_ref, embq_ref, unitq_ref, lenq_ref, sumq_ref,
    xq, xc, win, wout, proj, woutp, normed, hidden, cpart, qpart, base, crecv, qrecv,
    load_sem, csend_sem, crecv_sem, qsend_sem, qrecv_sem,
):
    ring = 8
    me = lax.axis_index("mp")
    right, left = lax.rem(me + 1, ring), lax.rem(me + ring - 1, ring)

    def home_of(i):
        even = 8 - (8 - i) // 2
        odd = (7 - i) // 2
        return lax.rem(me + jnp.where(lax.rem(i, 2) == 0, even, odd), ring)

    def load_x(i):
        rows = pl.ds(pl.multiple_of(home_of(jnp.int32(i)) * 256, 256), 256)
        return pltpu.make_async_copy(c_hbm.at[rows], xc.at[i], load_sem.at[i])

    loads = [
        pltpu.make_async_copy(q_hbm, xq, load_sem.at[8]),
        pltpu.make_async_copy(win_hbm, win, load_sem.at[9]),
        pltpu.make_async_copy(wout_hbm, wout, load_sem.at[10]),
        pltpu.make_async_copy(proj_hbm, proj, load_sem.at[11]),
    ]
    for load in loads:
        load.start()
    for i in range(8):
        load_x(i).start()

    barrier = pltpu.get_barrier_semaphore()
    for neighbour in (left, right):
        pl.semaphore_signal(barrier, inc=1, device_id={"mp": neighbour}, device_id_type=MESH)

    def normalise(src):
        @pl.loop(0, 8)
        def _(r):
            rows = pl.ds(pl.multiple_of(r * 32, 32), 32)
            v = src[rows, :].astype(f32)
            scale = lax.rsqrt(jnp.mean(v * v, axis=-1, keepdims=True) + norm_eps)
            normed[rows, :] = (v * scale * gain_ref[...]).astype(bf16)

    def feed():
        for n in range(2):
            gate = jnp.dot(normed[...], win[:, n * 256:(n + 1) * 256], preferred_element_type=f32)
            upper = jnp.dot(normed[...], win[:, 512 + n * 256:768 + n * 256], preferred_element_type=f32)
            hidden[:, n * 256:(n + 1) * 256] = (gate / (1.0 + jnp.exp(-gate)) * upper).astype(bf16)

    loads[0].wait()
    normalise(xq)
    loads[1].wait()
    feed()
    loads[2].wait()
    mixed_q = jnp.dot(hidden[...], wout[...], preferred_element_type=f32).astype(bf16)
    normed[...] = mixed_q
    for i in range(8):
        h = home_of(jnp.int32(i))
        qpart[i] = normed[pl.ds(pl.multiple_of(h * 32, 32), 32), :]
    loads[3].wait()
    woutp[...] = jnp.dot(wout[...], proj[...], preferred_element_type=f32).astype(bf16)
    pl.semaphore_wait(barrier, 2)

    def copies(way, u):
        first = way
        if u == 0:
            dist, half = 4, first
        elif u % 2 == 1:
            dist, half = 4 - (u + 1) // 2, 1 - first
        else:
            dist, half = 4 - u // 2, first
        i = part_of(way, dist)
        target = {"mp": right if way == 0 else left}
        crows, qrows = pl.ds(half * 128, 128), pl.ds(half * 16, 16)
        return (i, crows, qrows,
            pltpu.make_async_remote_copy(
                src_ref=cpart.at[i, crows], dst_ref=crecv.at[way, u], send_sem=csend_sem.at[way, u],
                recv_sem=crecv_sem.at[way, u], device_id=target, device_id_type=MESH),
            pltpu.make_async_remote_copy(
                src_ref=qpart.at[i, qrows], dst_ref=qrecv.at[way, u], send_sem=qsend_sem.at[way, u],
                recv_sem=qrecv_sem.at[way, u], device_id=target, device_id_type=MESH))

    def unit(way, u):
        i, crows, qrows, ccopy, qcopy = copies(way, u)
        if u >= 2:
            _, _, _, cbefore, qbefore = copies(way, u - 2)
            qbefore.wait_recv()
            qpart[i, qrows] = (qpart[i, qrows].astype(f32) + qrecv[way, u - 2].astype(f32)).astype(bf16)
            cbefore.wait_recv()
            cpart[i, crows] = (cpart[i, crows].astype(f32) + crecv[way, u - 2].astype(f32)).astype(bf16)
        ccopy.start()
        qcopy.start()

    @pl.loop(0, 8)
    def _(i):
        load_x(i).wait()
        normalise(xc.at[i])
        feed()
        cpart[i] = jnp.dot(hidden[...], woutp[...], preferred_element_type=f32).astype(bf16)

        @pl.when(i == 0)
        def _():
            unit(0, 0)
            unit(1, 0)

        @pl.when(i == 1)
        def _():
            unit(0, 1)

        @pl.when(i == 2)
        def _():
            unit(1, 1)

        @pl.when(i == 4)
        def _():
            unit(0, 2)
            unit(1, 2)

    for u in (3, 4):
        for way in (0, 1):
            unit(way, u)
    base[...] = jnp.dot(xc[7], proj[...], preferred_element_type=f32) + cpart[7].astype(f32)
    for u in (5, 6):
        for way in (0, 1):
            unit(way, u)

    for way in (0, 1):
        for u in (5, 6):
            _, _, _, ccopy, qcopy = copies(way, u)
            qcopy.wait_recv()
            ccopy.wait_recv()
    for half in range(2):
        ua, ub = (6, 5) if half == 0 else (5, 6)
        for r in range(0, 128, 64):
            rows = slice(half * 128 + r, half * 128 + r + 64)
            raw = base[rows, :] + crecv[0, ua, r:r + 64, :].astype(f32) + crecv[1, ub, r:r + 64, :].astype(f32)
            inverse = lax.rsqrt(jnp.sum(raw * raw, axis=-1, keepdims=True) + embed_eps)
            embc_ref[rows, :] = (raw * inverse).astype(bf16)
        qrows = slice(half * 16, half * 16 + 16)
        own = xq[pl.ds(pl.multiple_of(me * 32 + half * 16, 16), 16), :].astype(f32)
        mixed = qpart[7, qrows, :].astype(f32) + qrecv[0, ua].astype(f32) + qrecv[1, ub].astype(f32)
        sumq_ref[qrows, :] = (own + mixed).astype(bf16)
    raw_q = jnp.dot(sumq_ref[...], proj[...], preferred_element_type=f32)
    length = jnp.sqrt(jnp.sum(raw_q * raw_q, axis=-1, keepdims=True) + embed_eps)
    unit_q = raw_q / length
    unitq_ref[...] = unit_q
    embq_ref[...] = unit_q.astype(bf16)
    lenq_ref[...] = jnp.broadcast_to(length, (32, 128))
    for way in (0, 1):
        for u in range(7):
            _, _, _, ccopy, qcopy = copies(way, u)
            ccopy.wait_send()
            qcopy.wait_send()


def encode(queries, clips, gain, win, wout, proj):
    any_spec = pl.BlockSpec(memory_space=pl.ANY)
    vmem = pl.BlockSpec(memory_space=pltpu.VMEM)
    sds = jax.ShapeDtypeStruct
    return pl.pallas_call(
        encode_kernel,
        out_shape=(
            sds((256, 768), bf16), sds((32, 768), bf16), sds((32, 768), f32), sds((32, 128), f32),
            sds((32, 1024), bf16),
        ),
        in_specs=[any_spec, any_spec, vmem, any_spec, any_spec, any_spec],
        out_specs=[vmem] * 5,
        scratch_shapes=[
            pltpu.VMEM((256, 1024), bf16),
            pltpu.VMEM((8, 256, 1024), bf16),
            pltpu.VMEM((1024, 1024), bf16),
            pltpu.VMEM((512, 1024), bf16),
            pltpu.VMEM((1024, 768), bf16),
            pltpu.VMEM((512, 768), bf16),
            pltpu.VMEM((256, 1024), bf16),
            pltpu.VMEM((256, 512), bf16),
            pltpu.VMEM((8, 256, 768), bf16),
            pltpu.VMEM((8, 32, 1024), bf16),
            pltpu.VMEM((256, 768), f32),
            pltpu.VMEM((2, 7, 128, 768), bf16),
            pltpu.VMEM((2, 7, 16, 1024), bf16),
            pltpu.SemaphoreType.DMA((12,)),
            pltpu.SemaphoreType.DMA((2, 7)),
            pltpu.SemaphoreType.DMA((2, 7)),
            pltpu.SemaphoreType.DMA((2, 7)),
            pltpu.SemaphoreType.DMA((2, 7)),
        ],
        compiler_params=pltpu.CompilerParams(
            collective_id=0, has_side_effects=True, vmem_limit_bytes=48 * 1024 * 1024),
        cost_estimate=pl.CostEstimate(flops=8_500_000_000, bytes_accessed=20_000_000, transcendentals=2_000_000),
        name="encode",
    )(queries, clips, gain, win, wout, proj)


def slots_of(owner_ids, owners):
    onehot = (owner_ids[:, None] == jnp.arange(owners, dtype=jnp.int32)[None, :]).astype(jnp.int32)
    return jnp.sum(jnp.cumsum(onehot, axis=0) * onehot, axis=-1) - 1


def per_device(
    queries, clips, norm_gain, w_in, w_out, proj, pos_row, neg_owner, neg_row, clip_dest
):
    width = queries.shape[1]
    query_rows = pos_row.shape[0]
    clip_rows = clip_dest.shape[0]
    clip_embed, query_embed, query_unit, query_length, query_summed = encode(
        queries, clips, norm_gain.reshape(1, width), w_in.reshape(width, -1), w_out, proj)
    query_length = query_length[:, :1]
    embed_width = clip_embed.shape[1]
    owners = lax.axis_size(("group", "dp"))
    destination = clip_dest[:, 0]
    cap_index = max(2, min(clip_rows, 2 * clip_rows // owners))
    place_index = destination * cap_index + slots_of(destination, owners)
    outgoing = (
        jnp.zeros((owners * cap_index, embed_width), jnp.bfloat16).at[place_index].set(clip_embed)
    )
    received = lax.all_to_all(
        outgoing.reshape(owners, cap_index, embed_width),
        ("group", "dp"),
        split_axis=0,
        concat_axis=0,
        tiled=True,
    )
    index_shard = received.reshape(owners * cap_index, embed_width)
    peers = lax.axis_size(("dp", "mp"))
    negatives = neg_owner.shape[1]
    cap_fetch = max(2, min(query_rows, 4 * query_rows * negatives // peers))
    flat_owner = neg_owner.reshape(-1)
    place_fetch = flat_owner * cap_fetch + slots_of(flat_owner, peers)
    wanted = jnp.zeros((peers * cap_fetch,), jnp.int32).at[place_fetch].set(neg_row.reshape(-1))
    fetched = lax.all_to_all(
        clip_embed[
            lax.all_to_all(
                wanted.reshape(peers, cap_fetch),
                ("dp", "mp"),
                split_axis=0,
                concat_axis=0,
                tiled=True,
            )
        ],
        ("dp", "mp"),
        split_axis=0,
        concat_axis=0,
        tiled=True,
    )
    negative_embed = fetched.reshape(peers * cap_fetch, embed_width)[place_fetch].reshape(
        query_rows, negatives, embed_width
    )
    positive_embed = clip_embed[pos_row]
    candidates = jnp.concatenate([positive_embed[:, None, :], negative_embed], axis=1).astype(
        jnp.float32
    )
    scores = score_scale * jnp.einsum("qe,qce->qc", query_embed.astype(jnp.float32), candidates)
    weights = jnp.exp(scores)
    total = jnp.sum(weights, axis=-1)
    losses = jnp.log(total) - scores[:, 0]
    probs = weights / total[:, None]
    dunit = score_scale * (jnp.einsum("qc,qce->qe", probs, candidates) - candidates[:, 0, :])
    along = jnp.sum(query_unit * dunit, axis=-1, keepdims=True)
    draw = ((dunit - query_unit * along) / query_length).astype(jnp.bfloat16)
    slices = lax.axis_size("mp")
    pieces = query_summed.reshape(query_rows, owners, slices, -1).transpose(2, 0, 1, 3)
    pieces = lax.all_to_all(
        pieces.reshape(slices, query_rows, -1), "mp", split_axis=0, concat_axis=0, tiled=True)
    draws = lax.all_gather(draw, "mp", axis=0, tiled=True)
    term = lax.dot_general(
        pieces.reshape(slices * query_rows, -1), draws, (((0,), (0,)), ((), ())),
        preferred_element_type=jnp.float32)
    shares = lax.all_to_all(
        term.reshape(owners, -1, embed_width), ("group", "dp"), split_axis=0, concat_axis=0, tiled=True)
    grad_proj = jnp.sum(shares, axis=0)
    return (losses, index_shard, grad_proj)


def solution(mesh):
    return jax.shard_map(
        per_device,
        mesh=mesh,
        in_specs=(
            P(("group", "dp"), None),
            P(("group", "dp"), None),
            P(),
            P(None, None, "mp"),
            P("mp", None),
            P(),
            P(("group", "dp", "mp")),
            P(("group", "dp", "mp"), None),
            P(("group", "dp", "mp"), None),
            P(("group", "dp", "mp"), None),
        ),
        out_specs=(
            P(("group", "dp", "mp")),
            P(("group", "dp", "mp"), None),
            P(("group", "dp", "mp"), None),
        ),
        check_vma=False,
    )
```

```python
import jax
import jax.numpy as jnp
from jax import lax
from jax.experimental import pallas as pl
from jax.experimental.pallas import tpu as pltpu
from jax.sharding import PartitionSpec as P

norm_eps = 1e-06
embed_eps = 1e-06
score_scale = 20.0
MESH = pl.DeviceIdType.MESH
f32 = jnp.float32
bf16 = jnp.bfloat16


def part_of(way, dist):
    return 0 if dist == 4 else 7 - 2 * dist + way


def encode_kernel(
    q_hbm, c_hbm, gain_ref, win_hbm, wout_hbm, proj_hbm,
    embc_ref, embq_ref, unitq_ref, lenq_ref, sumq_ref,
    xq, xc, win, wout, proj, woutp, normed, hidden, cpart, qpart, base, crecv, qrecv,
    load_sem, csend_sem, crecv_sem, qsend_sem, qrecv_sem,
):
    ring = 8
    me = lax.axis_index("mp")
    right, left = lax.rem(me + 1, ring), lax.rem(me + ring - 1, ring)

    def home_of(i):
        even = 8 - (8 - i) // 2
        odd = (7 - i) // 2
        return lax.rem(me + jnp.where(lax.rem(i, 2) == 0, even, odd), ring)

    def load_x(i):
        rows = pl.ds(pl.multiple_of(home_of(jnp.int32(i)) * 256, 256), 256)
        return pltpu.make_async_copy(c_hbm.at[rows], xc.at[i], load_sem.at[i])

    loads = [
        pltpu.make_async_copy(q_hbm, xq, load_sem.at[8]),
        pltpu.make_async_copy(win_hbm, win, load_sem.at[9]),
        pltpu.make_async_copy(wout_hbm, wout, load_sem.at[10]),
        pltpu.make_async_copy(proj_hbm, proj, load_sem.at[11]),
    ]
    for load in loads:
        load.start()
    for i in range(8):
        load_x(i).start()

    barrier = pltpu.get_barrier_semaphore()
    for neighbour in (left, right):
        pl.semaphore_signal(barrier, inc=1, device_id={"mp": neighbour}, device_id_type=MESH)

    def normalise(src):
        @pl.loop(0, 8)
        def _(r):
            rows = pl.ds(pl.multiple_of(r * 32, 32), 32)
            v = src[rows, :].astype(f32)
            scale = lax.rsqrt(jnp.mean(v * v, axis=-1, keepdims=True) + norm_eps)
            normed[rows, :] = (v * scale * gain_ref[...]).astype(bf16)

    def feed():
        for n in range(2):
            gate = jnp.dot(normed[...], win[:, n * 256:(n + 1) * 256], preferred_element_type=f32)
            upper = jnp.dot(normed[...], win[:, 512 + n * 256:768 + n * 256], preferred_element_type=f32)
            hidden[:, n * 256:(n + 1) * 256] = (gate / (1.0 + jnp.exp(-gate)) * upper).astype(bf16)

    loads[0].wait()
    normalise(xq)
    loads[1].wait()
    feed()
    loads[2].wait()
    mixed_q = jnp.dot(hidden[...], wout[...], preferred_element_type=f32).astype(bf16)
    normed[...] = mixed_q
    for i in range(8):
        h = home_of(jnp.int32(i))
        qpart[i] = normed[pl.ds(pl.multiple_of(h * 32, 32), 32), :]
    loads[3].wait()
    woutp[...] = jnp.dot(wout[...], proj[...], preferred_element_type=f32).astype(bf16)
    pl.semaphore_wait(barrier, 2)

    def copies(way, u):
        first = way
        if u == 0:
            dist, half = 4, first
        elif u % 2 == 1:
            dist, half = 4 - (u + 1) // 2, 1 - first
        else:
            dist, half = 4 - u // 2, first
        i = part_of(way, dist)
        target = {"mp": right if way == 0 else left}
        crows, qrows = pl.ds(half * 128, 128), pl.ds(half * 16, 16)
        return (i, crows, qrows,
            pltpu.make_async_remote_copy(
                src_ref=cpart.at[i, crows], dst_ref=crecv.at[way, u], send_sem=csend_sem.at[way, u],
                recv_sem=crecv_sem.at[way, u], device_id=target, device_id_type=MESH),
            pltpu.make_async_remote_copy(
                src_ref=qpart.at[i, qrows], dst_ref=qrecv.at[way, u], send_sem=qsend_sem.at[way, u],
                recv_sem=qrecv_sem.at[way, u], device_id=target, device_id_type=MESH))

    def unit(way, u):
        i, crows, qrows, ccopy, qcopy = copies(way, u)
        if u >= 2:
            _, _, _, cbefore, qbefore = copies(way, u - 2)
            qbefore.wait_recv()
            qpart[i, qrows] = (qpart[i, qrows].astype(f32) + qrecv[way, u - 2].astype(f32)).astype(bf16)
            cbefore.wait_recv()
            cpart[i, crows] = (cpart[i, crows].astype(f32) + crecv[way, u - 2].astype(f32)).astype(bf16)
        ccopy.start()
        qcopy.start()

    @pl.loop(0, 8)
    def _(i):
        load_x(i).wait()
        normalise(xc.at[i])
        feed()
        cpart[i] = jnp.dot(hidden[...], woutp[...], preferred_element_type=f32).astype(bf16)

        @pl.when(i == 0)
        def _():
            unit(0, 0)
            unit(1, 0)

        @pl.when(i == 1)
        def _():
            unit(0, 1)

        @pl.when(i == 2)
        def _():
            unit(1, 1)

        @pl.when(i == 4)
        def _():
            unit(0, 2)
            unit(1, 2)

    for u in (3, 4):
        for way in (0, 1):
            unit(way, u)
    base[...] = jnp.dot(xc[7], proj[...], preferred_element_type=f32) + cpart[7].astype(f32)
    for u in (5, 6):
        for way in (0, 1):
            unit(way, u)

    for way in (0, 1):
        for u in (5, 6):
            _, _, _, ccopy, qcopy = copies(way, u)
            qcopy.wait_recv()
            ccopy.wait_recv()
    for half in range(2):
        ua, ub = (6, 5) if half == 0 else (5, 6)
        for r in range(0, 128, 64):
            rows = slice(half * 128 + r, half * 128 + r + 64)
            raw = base[rows, :] + crecv[0, ua, r:r + 64, :].astype(f32) + crecv[1, ub, r:r + 64, :].astype(f32)
            inverse = lax.rsqrt(jnp.sum(raw * raw, axis=-1, keepdims=True) + embed_eps)
            embc_ref[rows, :] = (raw * inverse).astype(bf16)
        qrows = slice(half * 16, half * 16 + 16)
        own = xq[pl.ds(pl.multiple_of(me * 32 + half * 16, 16), 16), :].astype(f32)
        mixed = qpart[7, qrows, :].astype(f32) + qrecv[0, ua].astype(f32) + qrecv[1, ub].astype(f32)
        sumq_ref[qrows, :] = (own + mixed).astype(bf16)
    raw_q = jnp.dot(sumq_ref[...], proj[...], preferred_element_type=f32)
    length = jnp.sqrt(jnp.sum(raw_q * raw_q, axis=-1, keepdims=True) + embed_eps)
    unit_q = raw_q / length
    unitq_ref[...] = unit_q
    embq_ref[...] = unit_q.astype(bf16)
    lenq_ref[...] = jnp.broadcast_to(length, (32, 128))
    for way in (0, 1):
        for u in range(7):
            _, _, _, ccopy, qcopy = copies(way, u)
            ccopy.wait_send()
            qcopy.wait_send()


def encode(queries, clips, gain, win, wout, proj):
    any_spec = pl.BlockSpec(memory_space=pl.ANY)
    vmem = pl.BlockSpec(memory_space=pltpu.VMEM)
    sds = jax.ShapeDtypeStruct
    return pl.pallas_call(
        encode_kernel,
        out_shape=(
            sds((256, 768), bf16), sds((32, 768), bf16), sds((32, 768), f32), sds((32, 128), f32),
            sds((32, 1024), bf16),
        ),
        in_specs=[any_spec, any_spec, vmem, any_spec, any_spec, any_spec],
        out_specs=[vmem] * 5,
        scratch_shapes=[
            pltpu.VMEM((256, 1024), bf16),
            pltpu.VMEM((8, 256, 1024), bf16),
            pltpu.VMEM((1024, 1024), bf16),
            pltpu.VMEM((512, 1024), bf16),
            pltpu.VMEM((1024, 768), bf16),
            pltpu.VMEM((512, 768), bf16),
            pltpu.VMEM((256, 1024), bf16),
            pltpu.VMEM((256, 512), bf16),
            pltpu.VMEM((8, 256, 768), bf16),
            pltpu.VMEM((8, 32, 1024), bf16),
            pltpu.VMEM((256, 768), f32),
            pltpu.VMEM((2, 7, 128, 768), bf16),
            pltpu.VMEM((2, 7, 16, 1024), bf16),
            pltpu.SemaphoreType.DMA((12,)),
            pltpu.SemaphoreType.DMA((2, 7)),
            pltpu.SemaphoreType.DMA((2, 7)),
            pltpu.SemaphoreType.DMA((2, 7)),
            pltpu.SemaphoreType.DMA((2, 7)),
        ],
        compiler_params=pltpu.CompilerParams(
            collective_id=0, has_side_effects=True, vmem_limit_bytes=48 * 1024 * 1024),
        cost_estimate=pl.CostEstimate(flops=8_500_000_000, bytes_accessed=20_000_000, transcendentals=2_000_000),
        name="encode",
    )(queries, clips, gain, win, wout, proj)


def exchange_kernel(
    embc_ref, embq_ref, unitq_ref, lenq_ref, sumq_ref, codes_ref, column_ref, idx_ref, pos_ref,
    loss_ref, grad_ref, index_ref,
    fetch, cands, qall, packed, slots, pieces, pieces_in, sums, sums_in, draw, draws, gshare, gshare_in,
    fetch_s, fetch_r, q_s, q_r, piece_s, piece_r, idx_s, idx_r, sums_s, sums_r, draw_s, draw_r, grad_s, grad_r,
):
    g, d, z = lax.axis_index("group"), lax.axis_index("dp"), lax.axis_index("mp")
    here = g * 16 + d

    def up(s):
        return lax.rem(z + s, 8)

    def across(s):
        return lax.rem(d + s, 16)

    def beyond(s):
        return lax.rem(here + s, 32)

    def plane(o):
        return {"group": o // 16, "dp": lax.rem(o, 16)}

    barrier = pltpu.get_barrier_semaphore()

    @pl.loop(1, 32)
    def _(s):
        pl.semaphore_signal(barrier, inc=1, device_id=plane(beyond(s)), device_id_type=MESH)

    @pl.loop(1, 8)
    def _(s):
        pl.semaphore_signal(barrier, inc=1, device_id={"mp": up(s)}, device_id_type=MESH)

    def remote(src, dst, send, recv, target):
        return pltpu.make_async_remote_copy(
            src_ref=src, dst_ref=dst, send_sem=send, recv_sem=recv, device_id=target, device_id_type=MESH)

    def q_copy(to, frm):
        return remote(embq_ref, qall.at[frm], q_s.at[to], q_r.at[frm], {"mp": to})

    def fetch_copy(to, frm):
        return remote(fetch.at[to], cands.at[:, frm], fetch_s.at[to], fetch_r.at[frm], {"dp": to})

    def piece_copy(to, frm):
        return remote(pieces.at[to], pieces_in.at[frm], piece_s.at[to], piece_r.at[frm], {"mp": to})

    def index_copy(to, frm):
        return remote(slots.at[to], index_ref.at[frm], idx_s.at[to], idx_r.at[frm], plane(to))

    def sums_copy(to, frm):
        return remote(sums.at[to], sums_in.at[frm], sums_s.at[to], sums_r.at[frm], {"mp": to})

    def draw_copy(to, frm):
        return remote(draw, draws.at[frm], draw_s.at[to], draw_r.at[frm], {"mp": to})

    def grad_copy(to, frm):
        return remote(gshare.at[to], gshare_in.at[frm], grad_s.at[to], grad_r.at[frm], plane(to))

    owner_slot = (d * 8 + z) * 8

    def pack(block):
        rank = lax.broadcasted_iota(jnp.int32, (8, 256), 0)
        for n in range(32):
            code = codes_ref[pl.ds(block * 32 + n, 1), :]
            hit = (code >> 8) == owner_slot + rank
            row = jnp.sum(jnp.where(hit, (code & 255) + 1, 0), axis=1, keepdims=True) - 1
            spot = lax.broadcasted_iota(jnp.int32, (8, 256), 1)
            packed[n * 8:(n + 1) * 8, :] = jnp.where(spot == row, 1.0, 0.0)
        rows = jnp.dot(packed[...].astype(bf16), embc_ref[...], preferred_element_type=f32).astype(bf16)
        for c in range(4):
            for part in range(4):
                fetch[block * 4 + c, part] = rows[c * 64 + part * 16:c * 64 + part * 16 + 16]

    y = d // 4
    pack(lax.rem(y + 1, 4))
    pl.semaphore_wait(barrier, 38)

    @pl.loop(1, 8)
    def _(s):
        q_copy(up(s), z).start()

    qall[z] = embq_ref[...]

    @pl.loop(0, 4)
    def _(s):
        block = lax.rem(y + 1 + s, 4)

        @pl.when(s > 0)
        def _():
            pack(block)

        @pl.loop(0, 4)
        def _(c):
            to = block * 4 + c

            @pl.when(to != d)
            def _():
                fetch_copy(to, d).start()

    cands[:, d] = fetch[d]

    @pl.loop(0, 2)
    def _(s):
        row = lax.broadcasted_iota(jnp.int32, (256, 256), 0) + s * 256
        onehot = jnp.where(row == idx_ref[...], 1.0, 0.0).astype(bf16)
        rows = jnp.dot(onehot, embc_ref[...], preferred_element_type=f32).astype(bf16)
        slots[pl.ds(s * 16, 16)] = rows.reshape(16, 16, 768)

    @pl.loop(0, 8)
    def _(s):
        m = up(s)
        source = lax.broadcasted_iota(jnp.int32, (1024, 256), 0)
        lane = lax.broadcasted_iota(jnp.int32, (1024, 256), 1)
        onehot = jnp.where(source == (lane >> 3) * 32 + m * 4 + (lane & 3), 1.0, 0.0).astype(bf16)
        pieces[m] = jnp.dot(sumq_ref[...], onehot, preferred_element_type=f32).astype(bf16)

        @pl.when(s > 0)
        def _():
            piece_copy(m, z).start()

    pieces_in[z] = pieces[z]
    unit = unitq_ref[...]
    length = lenq_ref[:, 0:1]
    at_pos = lax.broadcasted_iota(jnp.int32, (32, 256), 1) == pos_ref[...]
    positive = jnp.dot(
        jnp.where(at_pos, 1.0, 0.0).astype(bf16), embc_ref[...], preferred_element_type=f32)
    pos_score = score_scale * jnp.sum(embq_ref[...].astype(f32) * positive, axis=1, keepdims=True)
    pos_weight = jnp.exp(pos_score)

    @pl.loop(1, 8)
    def _(s):
        q_copy(z, up(s)).wait_recv()

    @pl.loop(1, 16)
    def _(s):
        fetch_copy(d, across(s)).wait_recv()

    @pl.loop(1, 32)
    def _(s):
        index_copy(beyond(s), here).start()

    own_index = pltpu.make_async_copy(slots.at[here], index_ref.at[here], idx_s.at[here])
    own_index.start()

    @pl.loop(0, 4)
    def _(s):
        pair = lax.rem(z // 2 + 1 + s, 4)
        q = qall[pl.ds(pair * 2, 2)].reshape(64, 768)
        cand = cands[pair].reshape(256, 768)
        score = score_scale * lax.dot_general(
            q, cand, (((1,), (1,)), ((), ())), preferred_element_type=f32)
        row = lax.broadcasted_iota(jnp.int32, (64, 256), 0)
        lane = lax.broadcasted_iota(jnp.int32, (64, 256), 1)
        slot = ((lane >> 4) * 8 + z) * 8 + (lane & 7)
        owned = column_ref[pl.ds(pl.multiple_of(pair * 64, 64), 64), :]
        hit = (owned[:, 0:1] >> 8) == slot
        for k in range(1, 8):
            hit = hit | ((owned[:, k:k + 1] >> 8) == slot)
        hit = hit & ((row >> 5) == ((lane >> 3) & 1))
        weight = jnp.where(hit, jnp.exp(score), 0.0)
        total = jnp.sum(weight, axis=1, keepdims=True)
        summed = jnp.dot(weight.astype(bf16), cand, preferred_element_type=f32).astype(bf16)
        high = total.astype(bf16)
        low = (total - high.astype(f32)).astype(bf16)
        first = lax.broadcasted_iota(jnp.int32, (64, 128), 1) < 64
        tail = jnp.where(first, high.astype(f32), low.astype(f32)).astype(bf16)
        for k in range(2):
            m = pair * 2 + k
            sums[m, :, 0:768] = summed[k * 32:(k + 1) * 32]
            sums[m, :, 768:896] = tail[k * 32:(k + 1) * 32]

            @pl.when(m != z)
            def _():
                sums_copy(m, z).start()

    sums_in[z] = sums[z]

    @pl.loop(1, 8)
    def _(s):
        sums_copy(z, up(s)).wait_recv()

    gathered = sums_in[0].astype(f32)
    for m in range(1, 8):
        gathered = gathered + sums_in[m].astype(f32)
    total = gathered[:, 768:769] + gathered[:, 832:833] + pos_weight
    loss = jnp.log(total) - pos_score
    diagonal = lax.broadcasted_iota(jnp.int32, (32, 32), 0) == lax.broadcasted_iota(jnp.int32, (32, 32), 1)
    loss_ref[...] = jnp.sum(jnp.where(diagonal, loss, 0.0), axis=0, keepdims=True)
    dunit = score_scale * ((gathered[:, 0:768] + pos_weight * positive) / total - positive)
    along = jnp.sum(unit * dunit, axis=1, keepdims=True)
    draw[...] = ((dunit - unit * along) / length).astype(bf16)

    @pl.loop(1, 8)
    def _(s):
        draw_copy(up(s), z).start()

    draws[z] = draw[...]

    @pl.loop(1, 8)
    def _(s):
        piece_copy(z, up(s)).wait_recv()

    @pl.loop(1, 8)
    def _(s):
        draw_copy(z, up(s)).wait_recv()

    term = lax.dot_general(
        pieces_in[...].reshape(256, 256), draws[...].reshape(256, 768), (((0,), (0,)), ((), ())),
        preferred_element_type=f32)
    upper = (lax.broadcasted_iota(jnp.int32, (256, 384), 0) & 7) < 4
    gshare[...] = jnp.where(upper, term[:, 0:384], term[:, 384:768]).reshape(32, 8, 384)

    @pl.loop(1, 32)
    def _(s):
        grad_copy(beyond(s), here).start()

    gshare_in[here] = gshare[here]

    @pl.loop(1, 32)
    def _(s):
        grad_copy(here, beyond(s)).wait_recv()

    grad = jnp.sum(gshare_in[...], axis=0)
    grad_ref[:, 0:384] = grad[0:4]
    grad_ref[:, 384:768] = grad[4:8]

    @pl.loop(1, 32)
    def _(s):
        index_copy(here, beyond(s)).wait_recv()

    own_index.wait()

    @pl.loop(1, 8)
    def _(s):
        q_copy(up(s), z).wait_send()
        piece_copy(up(s), z).wait_send()
        sums_copy(up(s), z).wait_send()
        draw_copy(up(s), z).wait_send()

    @pl.loop(1, 16)
    def _(s):
        fetch_copy(across(s), d).wait_send()

    @pl.loop(1, 32)
    def _(s):
        index_copy(beyond(s), here).wait_send()
        grad_copy(beyond(s), here).wait_send()


def exchange(embc, embq, unitq, lenq, sumq, codes, column, idx, pos):
    vmem = pl.BlockSpec(memory_space=pltpu.VMEM)
    sds = jax.ShapeDtypeStruct
    dma = pltpu.SemaphoreType.DMA
    return pl.pallas_call(
        exchange_kernel,
        out_shape=(sds((1, 32), f32), sds((4, 768), f32), sds((32, 16, 768), bf16)),
        in_specs=[vmem] * 9,
        out_specs=[vmem, vmem, pl.BlockSpec(memory_space=pl.ANY)],
        scratch_shapes=[
            pltpu.VMEM((16, 4, 16, 768), bf16),
            pltpu.VMEM((4, 16, 16, 768), bf16),
            pltpu.VMEM((8, 32, 768), bf16),
            pltpu.VMEM((256, 256), f32),
            pltpu.VMEM((32, 16, 768), bf16),
            pltpu.VMEM((8, 32, 256), bf16),
            pltpu.VMEM((8, 32, 256), bf16),
            pltpu.VMEM((8, 32, 896), bf16),
            pltpu.VMEM((8, 32, 896), bf16),
            pltpu.VMEM((32, 768), bf16),
            pltpu.VMEM((8, 32, 768), bf16),
            pltpu.VMEM((32, 8, 384), f32),
            pltpu.VMEM((32, 8, 384), f32),
            dma((16,)), dma((16,)), dma((8,)), dma((8,)), dma((8,)), dma((8,)), dma((32,)), dma((32,)),
            dma((8,)), dma((8,)), dma((8,)), dma((8,)), dma((32,)), dma((32,)),
        ],
        compiler_params=pltpu.CompilerParams(
            collective_id=1, has_side_effects=True, vmem_limit_bytes=48 * 1024 * 1024),
        cost_estimate=pl.CostEstimate(flops=2_500_000_000, bytes_accessed=4_000_000, transcendentals=100_000),
        name="exchange",
    )(embc, embq, unitq, lenq, sumq, codes, column, idx, pos)


def ranks_of(ids):
    count = ids.shape[0]
    earlier = jnp.arange(count)[None, :] < jnp.arange(count)[:, None]
    return jnp.sum(((ids[:, None] == ids[None, :]) & earlier).astype(jnp.int32), axis=1)


def per_device(
    queries, clips, norm_gain, w_in, w_out, proj, pos_row, neg_owner, neg_row, clip_dest
):
    width = queries.shape[1]
    asked = neg_owner.reshape(-1)
    code = (asked * 8 + ranks_of(asked)) * 256 + neg_row.reshape(-1)
    codes = lax.all_gather(code, ("dp", "mp"), axis=0, tiled=False)
    destination = clip_dest[:, 0]
    idx = (destination * 16 + ranks_of(destination)).reshape(1, -1)
    embc, embq, unitq, lenq, sumq = encode(
        queries, clips, norm_gain.reshape(1, width), w_in.reshape(width, -1), w_out, proj)
    column = lax.dynamic_slice_in_dim(codes, lax.axis_index("dp") * 8, 8, 0).reshape(256, 8)
    loss, grad, index = exchange(
        embc, embq, unitq, lenq, sumq, codes, column, idx, pos_row.reshape(-1, 1))
    return (loss.reshape(-1), index.reshape(-1, index.shape[-1]), grad)


def solution(mesh):
    return jax.shard_map(
        per_device,
        mesh=mesh,
        in_specs=(
            P(("group", "dp"), None),
            P(("group", "dp"), None),
            P(),
            P(None, None, "mp"),
            P("mp", None),
            P(),
            P(("group", "dp", "mp")),
            P(("group", "dp", "mp"), None),
            P(("group", "dp", "mp"), None),
            P(("group", "dp", "mp"), None),
        ),
        out_specs=(
            P(("group", "dp", "mp")),
            P(("group", "dp", "mp"), None),
            P(("group", "dp", "mp"), None),
        ),
        check_vma=False,
    )
```

```python
import jax
import jax.numpy as jnp
from jax import lax
from jax.experimental import pallas as pl
from jax.experimental.pallas import tpu as pltpu
from jax.sharding import PartitionSpec as P

norm_eps = 1e-06
embed_eps = 1e-06
score_scale = 20.0
MESH = pl.DeviceIdType.MESH
f32 = jnp.float32
bf16 = jnp.bfloat16
FAR_FIRST = (
    (2, 2), (3, 2), (2, 3), (2, 1), (1, 2), (3, 1), (1, 3), (3, 3), (1, 1), (0, 2), (2, 0), (3, 0), (0, 3), (1, 0),
    (0, 1),
)


def part_of(way, dist):
    return 0 if dist == 4 else 8 - 2 * dist + way


def kernel(
    q_hbm, c_hbm, gain_ref, win_hbm, wout_hbm, proj_hbm, code_ref, mine_ref, idx_ref, pos_ref,
    loss_ref, grad_ref, index_ref,
    x, win, wout, proj, woutp, normed, hidden, cpart, qpart, base, crecv, qrecv,
    codes, column, onehots, packed, embc, embq, sumq,
    fetch, cands, qall, slots, pieces, pieces_in, sums, sums_in, draw, draws, gshare, gshare_in,
    load_sem, c_s, c_r, qp_s, qp_r, code_s, code_r, col_s, col_r, plane_s, plane_r,
    fetch_s, fetch_r, q_s, q_r, piece_s, piece_r, idx_s, idx_r, sums_s, sums_r, draw_s, draw_r, grad_s, grad_r,
):
    g, d, z = lax.axis_index("group"), lax.axis_index("dp"), lax.axis_index("mp")
    y, xx = d // 4, lax.rem(d, 4)
    here = g * 16 + d
    right, left = lax.rem(z + 1, 8), lax.rem(z + 7, 8)

    def up(s):
        return lax.rem(z + s, 8)

    def across(dy, dx):
        return lax.rem(y + dy, 4) * 4 + lax.rem(xx + dx, 4)

    def owner(o):
        return {"group": o // 16, "dp": lax.rem(o, 16)}

    def remote(src, dst, send, recv, target):
        return pltpu.make_async_remote_copy(
            src_ref=src, dst_ref=dst, send_sem=send, recv_sem=recv, device_id=target, device_id_type=MESH)

    def home_of(i):
        even = (8 - i) // 2
        odd = 8 - (9 - i) // 2
        return lax.rem(z + jnp.where(lax.rem(i, 2) == 0, even, odd), 8)

    def load_x(i):
        rows = pl.ds(pl.multiple_of(home_of(jnp.int32(i)) * 256, 256), 256)
        return pltpu.make_async_copy(c_hbm.at[rows], x.at[i], load_sem.at[i])

    load_q = pltpu.make_async_copy(q_hbm, x.at[1], load_sem.at[1])
    load_in = pltpu.make_async_copy(win_hbm, win, load_sem.at[9])
    load_out = pltpu.make_async_copy(wout_hbm, wout, load_sem.at[10])
    load_proj = pltpu.make_async_copy(proj_hbm, proj, load_sem.at[11])
    load_x(0).start()
    load_out.start()
    load_proj.start()
    load_in.start()
    load_q.start()
    for i in range(2, 9):
        load_x(i).start()

    barrier = pltpu.get_barrier_semaphore()

    @pl.loop(1, 32)
    def _(s):
        pl.semaphore_signal(barrier, inc=1, device_id=owner(lax.rem(here + s, 32)), device_id_type=MESH)

    @pl.loop(1, 8)
    def _(s):
        pl.semaphore_signal(barrier, inc=1, device_id={"mp": up(s)}, device_id_type=MESH)

    def code_copy(to, frm):
        return remote(code_ref.at[0], codes.at[d, frm], code_s.at[to], code_r.at[frm], {"mp": to})

    def column_copy(to, frm):
        return remote(mine_ref, column.at[frm], col_s.at[to], col_r.at[frm], {"mp": to})

    def plane_copy(to, frm):
        return remote(codes.at[frm], codes.at[frm], plane_s.at[to], plane_r.at[frm], {"dp": to})

    def q_copy(to, frm):
        return remote(embq, qall.at[frm], q_s.at[to], q_r.at[frm], {"mp": to})

    def fetch_copy(pair, to, frm):
        return remote(
            fetch.at[pair, to], cands.at[pair, frm], fetch_s.at[pair, to], fetch_r.at[pair, frm], {"dp": to})

    def piece_copy(to, frm):
        return remote(pieces.at[to // 2], pieces_in.at[frm], piece_s.at[to], piece_r.at[frm], {"mp": to})

    def index_copy(to, frm):
        return remote(slots.at[to], index_ref.at[frm], idx_s.at[to], idx_r.at[frm], owner(to))

    def sums_copy(to, frm):
        return remote(sums.at[to], sums_in.at[frm], sums_s.at[to], sums_r.at[frm], {"mp": to})

    def draw_copy(to, frm):
        return remote(draw, draws.at[frm], draw_s.at[to], draw_r.at[frm], {"mp": to})

    def grad_copy(to, frm):
        return remote(gshare.at[to], gshare_in.at[frm], grad_s.at[to], grad_r.at[frm], owner(to))

    def spot(way, u):
        if u == 0:
            dist, half = 4, way
        elif u % 2 == 1:
            dist, half = 4 - (u + 1) // 2, 1 - way
        else:
            dist, half = 4 - u // 2, way
        return part_of(way, dist), slice(half * 128, half * 128 + 128), slice(half * 16, half * 16 + 16)

    def c_copy(way, u):
        i, rows, _ = spot(way, u)
        return remote(
            cpart.at[i, rows], crecv.at[way, u], c_s.at[way, u], c_r.at[way, u],
            {"mp": right if way == 0 else left})

    def qp_copy(way, u):
        i, _, rows = spot(way, u)
        return remote(
            qpart.at[i, rows], qrecv.at[way, u], qp_s.at[way, u], qp_r.at[way, u],
            {"mp": right if way == 0 else left})

    def q_unit(way, u):
        i, _, rows = spot(way, u)
        if u >= 2:
            qp_copy(way, u - 2).wait_recv()
            qpart[i, rows] = (qpart[i, rows].astype(f32) + qrecv[way, u - 2].astype(f32)).astype(bf16)
        qp_copy(way, u).start()

    def c_unit(way, u):
        i, rows, _ = spot(way, u)
        if u >= 2:
            c_copy(way, u - 2).wait_recv()
            cpart[i, rows] = (cpart[i, rows].astype(f32) + crecv[way, u - 2].astype(f32)).astype(bf16)
        c_copy(way, u).start()

    def both_units(u):
        q_unit(0, u)
        q_unit(1, u)
        c_unit(0, u)
        c_unit(1, u)

    load_out.wait()
    load_proj.wait()
    woutp[...] = jnp.dot(wout[...], proj[...], preferred_element_type=f32).astype(bf16)

    @pl.loop(0, 9)
    def _(i):
        @pl.when(i == 1)
        def _():
            load_q.wait()

        @pl.when(i != 1)
        def _():
            load_x(i).wait()

        @pl.loop(0, 8)
        def _(r):
            rows = pl.ds(pl.multiple_of(r * 32, 32), 32)
            v = x[i, rows, :].astype(f32)
            scale = lax.rsqrt(jnp.mean(v * v, axis=-1, keepdims=True) + norm_eps)
            normed[rows, :] = (v * scale * gain_ref[...]).astype(bf16)

        @pl.when(i == 0)
        def _():
            load_in.wait()

        for n in range(2):
            gate = jnp.dot(normed[...], win[:, n * 256:(n + 1) * 256], preferred_element_type=f32)
            upper = jnp.dot(normed[...], win[:, 512 + n * 256:768 + n * 256], preferred_element_type=f32)
            hidden[:, n * 256:(n + 1) * 256] = (gate / (1.0 + jnp.exp(-gate)) * upper).astype(bf16)

        @pl.when(i == 0)
        def _():
            pl.semaphore_wait(barrier, 38)

        @pl.when(i == 1)
        def _():
            normed[...] = jnp.dot(hidden[...], wout[...], preferred_element_type=f32).astype(bf16)
            for k in (0, 2, 3, 4, 5, 6, 7, 8):
                h = home_of(jnp.int32(k))
                qpart[k] = normed[pl.ds(pl.multiple_of(h * 32, 32), 32), :]
            q_unit(0, 0)
            q_unit(1, 0)

        @pl.when(i != 1)
        def _():
            cpart[i] = jnp.dot(hidden[...], woutp[...], preferred_element_type=f32).astype(bf16)

        @pl.when(i == 0)
        def _():
            c_unit(0, 0)
            c_unit(1, 0)

            @pl.loop(1, 8)
            def _(s):
                code_copy(up(s), z).start()
                column_copy(up(s), z).start()

            codes[d, z] = code_ref[0]
            column[z] = mine_ref[...]

        @pl.when(i == 2)
        def _():
            q_unit(0, 1)
            c_unit(0, 1)

        @pl.when(i == 3)
        def _():
            q_unit(1, 1)
            c_unit(1, 1)

        @pl.when(i == 5)
        def _():
            both_units(2)

        @pl.when(i == 6)
        def _():
            @pl.loop(1, 8)
            def _(s):
                code_copy(z, up(s)).wait_recv()
                column_copy(z, up(s)).wait_recv()

            @pl.loop(1, 16)
            def _(s):
                plane_copy(lax.rem(d + s, 16), d).start()

    both_units(3)
    base[...] = jnp.dot(x[8], proj[...], preferred_element_type=f32) + cpart[8].astype(f32)

    @pl.loop(1, 16)
    def _(s):
        plane_copy(d, lax.rem(d + s, 16)).wait_recv()

    owner_slot = (d * 8 + z) * 8

    def wanted(pair):
        rank = lax.broadcasted_iota(jnp.int32, (8, 256), 0)
        lane = lax.broadcasted_iota(jnp.int32, (8, 256), 1)
        for c in range(16):
            for k in range(2):
                code = codes[c, pair * 2 + k]
                hit = (code >> 8) == owner_slot + rank
                row = jnp.sum(jnp.where(hit, (code & 255) + 1, 0), axis=1, keepdims=True) - 1
                packed[c * 16 + k * 8:c * 16 + k * 8 + 8, :] = jnp.where(lane == row, 1.0, 0.0)
        onehots[pair] = packed[...].astype(bf16)

    @pl.loop(0, 2)
    def _(pair):
        wanted(pair)

    both_units(4)

    @pl.loop(2, 4)
    def _(pair):
        wanted(pair)

    both_units(5)
    both_units(6)

    for way in (0, 1):
        for u in (5, 6):
            qp_copy(way, u).wait_recv()
    for half in range(2):
        rows = slice(half * 16, half * 16 + 16)
        own = x[1, pl.ds(pl.multiple_of(z * 32 + half * 16, 16), 16), :].astype(f32)
        mixed = (
            qpart[8, rows].astype(f32) + qrecv[0, 6 - half].astype(f32) + qrecv[1, 5 + half].astype(f32))
        sumq[rows, :] = (own + mixed).astype(bf16)
    raw = jnp.dot(sumq[...], proj[...], preferred_element_type=f32)
    length = jnp.sqrt(jnp.sum(raw * raw, axis=-1, keepdims=True) + embed_eps)
    unit = raw / length
    embq[...] = unit.astype(bf16)
    qall[z] = embq[...]
    for s in (6, 7, 5, 4, 3, 2, 1):
        q_copy(up(s), z).start()

    for way in (0, 1):
        for u in (5, 6):
            c_copy(way, u).wait_recv()
    for half in range(2):
        for r in range(0, 128, 64):
            rows = slice(half * 128 + r, half * 128 + r + 64)
            raw_c = (
                base[rows, :] + crecv[0, 6 - half, r:r + 64].astype(f32)
                + crecv[1, 5 + half, r:r + 64].astype(f32))
            inverse = lax.rsqrt(jnp.sum(raw_c * raw_c, axis=-1, keepdims=True) + embed_eps)
            embc[rows, :] = (raw_c * inverse).astype(bf16)

    def pair_at(s):
        return lax.rem(z // 2 + 1 + s, 4)

    @pl.loop(0, 4)
    def _(s):
        pair = pair_at(s)
        rows = jnp.dot(onehots[pair], embc[...], preferred_element_type=f32).astype(bf16)
        fetch[pair] = rows.reshape(16, 16, 768)
        for dy, dx in FAR_FIRST:
            fetch_copy(pair, across(dy, dx), d).start()
        cands[pair, d] = fetch[pair, d]

    turned = sumq[...].astype(f32).T.reshape(32, 4, 8, 32)
    for k in range(4):
        pieces[k] = turned[:, k].reshape(256, 32).T.astype(bf16)

    @pl.loop(1, 8)
    def _(s):
        piece_copy(up(s), z).start()

    pieces_in[z] = pieces[z // 2]

    @pl.loop(0, 2)
    def _(s):
        row = lax.broadcasted_iota(jnp.int32, (256, 256), 0) + s * 256
        onehot = jnp.where(row == idx_ref[...], 1.0, 0.0).astype(bf16)
        rows = jnp.dot(onehot, embc[...], preferred_element_type=f32).astype(bf16)
        slots[pl.ds(s * 16, 16)] = rows.reshape(16, 16, 768)

    at_pos = lax.broadcasted_iota(jnp.int32, (32, 256), 1) == pos_ref[...]
    positive = jnp.dot(jnp.where(at_pos, 1.0, 0.0).astype(bf16), embc[...], preferred_element_type=f32)
    pos_score = score_scale * jnp.sum(embq[...].astype(f32) * positive, axis=1, keepdims=True)
    pos_weight = jnp.exp(pos_score)

    @pl.loop(0, 4)
    def _(s):
        pair = pair_at(s)
        for k in range(2):
            @pl.when(pair * 2 + k != z)
            def _():
                q_copy(z, pair * 2 + k).wait_recv()

        @pl.loop(1, 16)
        def _(t):
            fetch_copy(pair, d, lax.rem(d + t, 16)).wait_recv()

        q = qall[pl.ds(pair * 2, 2)].reshape(64, 768)
        cand = cands[pair].reshape(256, 768)
        score = score_scale * lax.dot_general(
            q, cand, (((1,), (1,)), ((), ())), preferred_element_type=f32)
        row = lax.broadcasted_iota(jnp.int32, (64, 256), 0)
        lane = lax.broadcasted_iota(jnp.int32, (64, 256), 1)
        slot = ((lane >> 4) * 8 + z) * 8 + (lane & 7)
        asked = column[pl.ds(pair * 2, 2)].reshape(64, 8)
        hit = (asked[:, 0:1] >> 8) == slot
        for k in range(1, 8):
            hit = hit | ((asked[:, k:k + 1] >> 8) == slot)
        hit = hit & ((row >> 5) == ((lane >> 3) & 1))
        weight = jnp.where(hit, jnp.exp(score), 0.0)
        total = jnp.sum(weight, axis=1, keepdims=True)
        summed = jnp.dot(weight.astype(bf16), cand, preferred_element_type=f32).astype(bf16)
        high = total.astype(bf16).astype(f32)
        first = lax.broadcasted_iota(jnp.int32, (64, 128), 1) < 64
        tail = jnp.where(first, high, total - high).astype(bf16)
        for k in range(2):
            sums[pair * 2 + k, :, 0:768] = summed[k * 32:(k + 1) * 32]
            sums[pair * 2 + k, :, 768:896] = tail[k * 32:(k + 1) * 32]

            @pl.when(pair * 2 + k != z)
            def _():
                sums_copy(pair * 2 + k, z).start()

    sums_in[z] = sums[z]
    own_index = pltpu.make_async_copy(slots.at[here], index_ref.at[here], idx_s.at[here])
    own_index.start()
    for dy, dx in FAR_FIRST:
        for k in range(2):
            index_copy(k * 16 + across(dy, dx), here).start()
    index_copy((1 - g) * 16 + d, here).start()

    @pl.loop(1, 8)
    def _(s):
        sums_copy(z, up(s)).wait_recv()

    gathered = sums_in[0].astype(f32)
    for m in range(1, 8):
        gathered = gathered + sums_in[m].astype(f32)
    total = gathered[:, 768:769] + gathered[:, 832:833] + pos_weight
    loss = jnp.log(total) - pos_score
    diagonal = lax.broadcasted_iota(jnp.int32, (32, 32), 0) == lax.broadcasted_iota(jnp.int32, (32, 32), 1)
    loss_ref[...] = jnp.sum(jnp.where(diagonal, loss, 0.0), axis=0, keepdims=True)
    dunit = score_scale * ((gathered[:, 0:768] + pos_weight * positive) / total - positive)
    along = jnp.sum(unit * dunit, axis=1, keepdims=True)
    draw[...] = ((dunit - unit * along) / length).astype(bf16)
    for s in (4, 3, 5, 2, 6, 1, 7):
        draw_copy(up(s), z).start()
    draws[z] = draw[...]

    @pl.loop(1, 8)
    def _(s):
        piece_copy(z, up(s)).wait_recv()

    @pl.loop(1, 8)
    def _(s):
        draw_copy(z, up(s)).wait_recv()

    term = lax.dot_general(
        pieces_in[...].reshape(256, 256), draws[...].reshape(256, 768), (((0,), (0,)), ((), ())),
        preferred_element_type=f32).reshape(32, 8, 768)
    turned_term = jnp.concatenate([term[:, 4:8], term[:, 0:4]], axis=1)
    even = lax.rem(z, 2) == 0
    upper_rows = lax.broadcasted_iota(jnp.int32, (32, 8, 384), 1) < 4
    gshare[...] = jnp.where(
        upper_rows,
        jnp.where(even, term[:, :, 0:384], turned_term[:, :, 0:384]),
        jnp.where(even, turned_term[:, :, 384:768], term[:, :, 384:768]))
    for dy, dx in FAR_FIRST:
        for k in range(2):
            grad_copy(k * 16 + across(dy, dx), here).start()
    grad_copy((1 - g) * 16 + d, here).start()
    gshare_in[here] = gshare[here]

    for way in (0, 1):
        for u in range(7):
            qp_copy(way, u).wait_send()
            c_copy(way, u).wait_send()

    @pl.loop(1, 8)
    def _(s):
        code_copy(up(s), z).wait_send()
        column_copy(up(s), z).wait_send()
        q_copy(up(s), z).wait_send()
        piece_copy(up(s), z).wait_send()
        sums_copy(up(s), z).wait_send()
        draw_copy(up(s), z).wait_send()

    @pl.loop(1, 16)
    def _(s):
        to = lax.rem(d + s, 16)
        plane_copy(to, d).wait_send()
        for pair in range(4):
            fetch_copy(pair, to, d).wait_send()

    own_index.wait()

    @pl.loop(1, 32)
    def _(s):
        other = lax.rem(here + s, 32)
        index_copy(other, here).wait_send()
        index_copy(here, other).wait_recv()

    @pl.loop(1, 32)
    def _(s):
        other = lax.rem(here + s, 32)
        grad_copy(other, here).wait_send()
        grad_copy(here, other).wait_recv()

    grad = jnp.sum(gshare_in[...], axis=0)
    grad_ref[:, 0:384] = grad[0:4]
    grad_ref[:, 384:768] = grad[4:8]


def fused(queries, clips, gain, win, wout, proj, code, mine, idx, pos):
    hbm = pl.BlockSpec(memory_space=pl.ANY)
    vmem = pl.BlockSpec(memory_space=pltpu.VMEM)
    sds = jax.ShapeDtypeStruct
    dma = pltpu.SemaphoreType.DMA
    return pl.pallas_call(
        kernel,
        out_shape=(sds((1, 32), f32), sds((4, 768), f32), sds((32, 16, 768), bf16)),
        in_specs=[hbm, hbm, vmem, hbm, hbm, hbm, vmem, vmem, vmem, vmem],
        out_specs=[vmem, vmem, hbm],
        scratch_shapes=[
            pltpu.VMEM((9, 256, 1024), bf16),
            pltpu.VMEM((1024, 1024), bf16),
            pltpu.VMEM((512, 1024), bf16),
            pltpu.VMEM((1024, 768), bf16),
            pltpu.VMEM((512, 768), bf16),
            pltpu.VMEM((256, 1024), bf16),
            pltpu.VMEM((256, 512), bf16),
            pltpu.VMEM((9, 256, 768), bf16),
            pltpu.VMEM((9, 32, 1024), bf16),
            pltpu.VMEM((256, 768), f32),
            pltpu.VMEM((2, 7, 128, 768), bf16),
            pltpu.VMEM((2, 7, 16, 1024), bf16),
            pltpu.VMEM((16, 8, 1, 256), jnp.int32),
            pltpu.VMEM((8, 32, 8), jnp.int32),
            pltpu.VMEM((4, 256, 256), bf16),
            pltpu.VMEM((256, 256), f32),
            pltpu.VMEM((256, 768), bf16),
            pltpu.VMEM((32, 768), bf16),
            pltpu.VMEM((32, 1024), bf16),
            pltpu.VMEM((4, 16, 16, 768), bf16),
            pltpu.VMEM((4, 16, 16, 768), bf16),
            pltpu.VMEM((8, 32, 768), bf16),
            pltpu.VMEM((32, 16, 768), bf16),
            pltpu.VMEM((4, 32, 256), bf16),
            pltpu.VMEM((8, 32, 256), bf16),
            pltpu.VMEM((8, 32, 896), bf16),
            pltpu.VMEM((8, 32, 896), bf16),
            pltpu.VMEM((32, 768), bf16),
            pltpu.VMEM((8, 32, 768), bf16),
            pltpu.VMEM((32, 8, 384), f32),
            pltpu.VMEM((32, 8, 384), f32),
            dma((12,)), dma((2, 7)), dma((2, 7)), dma((2, 7)), dma((2, 7)), dma((8,)), dma((8,)), dma((8,)), dma((8,)),
            dma((16,)), dma((16,)), dma((4, 16)), dma((4, 16)), dma((8,)), dma((8,)), dma((8,)), dma((8,)),
            dma((32,)), dma((32,)), dma((8,)), dma((8,)), dma((8,)), dma((8,)), dma((32,)), dma((32,)),
        ],
        compiler_params=pltpu.CompilerParams(
            collective_id=0, has_side_effects=True, vmem_limit_bytes=52 * 1024 * 1024),
        cost_estimate=pl.CostEstimate(flops=11_000_000_000, bytes_accessed=20_000_000, transcendentals=2_000_000),
        name="fused",
    )(queries, clips, gain, win, wout, proj, code, mine, idx, pos)


def ranks_of(ids):
    count = ids.shape[0]
    earlier = jnp.arange(count)[None, :] < jnp.arange(count)[:, None]
    return jnp.sum(((ids[:, None] == ids[None, :]) & earlier).astype(jnp.int32), axis=1)


def per_device(
    queries, clips, norm_gain, w_in, w_out, proj, pos_row, neg_owner, neg_row, clip_dest
):
    width = queries.shape[1]
    asked = neg_owner.reshape(-1)
    code = (asked * 8 + ranks_of(asked)) * 256 + neg_row.reshape(-1)
    destination = clip_dest[:, 0]
    idx = destination * 16 + ranks_of(destination)
    loss, grad, index = fused(
        queries, clips, norm_gain.reshape(1, width), w_in.reshape(width, -1), w_out, proj,
        code.reshape(1, 1, -1), code.reshape(neg_owner.shape), idx.reshape(1, -1), pos_row.reshape(-1, 1))
    return (loss.reshape(-1), index.reshape(-1, index.shape[-1]), grad)


def solution(mesh):
    return jax.shard_map(
        per_device,
        mesh=mesh,
        in_specs=(
            P(("group", "dp"), None),
            P(("group", "dp"), None),
            P(),
            P(None, None, "mp"),
            P("mp", None),
            P(),
            P(("group", "dp", "mp")),
            P(("group", "dp", "mp"), None),
            P(("group", "dp", "mp"), None),
            P(("group", "dp", "mp"), None),
        ),
        out_specs=(
            P(("group", "dp", "mp")),
            P(("group", "dp", "mp"), None),
            P(("group", "dp", "mp"), None),
        ),
        check_vma=False,
    )
```

```python
import jax
import jax.numpy as jnp
from jax import lax
from jax.experimental import pallas as pl
from jax.experimental.pallas import tpu as pltpu
from jax.sharding import PartitionSpec as P

norm_eps = 1e-06
embed_eps = 1e-06
score_scale = 20.0
MESH = pl.DeviceIdType.MESH
f32 = jnp.float32
bf16 = jnp.bfloat16
FAR_FIRST = (
    (2, 2), (3, 2), (2, 3), (2, 1), (1, 2), (3, 1), (1, 3), (3, 3), (1, 1), (0, 2), (2, 0), (3, 0), (0, 3), (1, 0),
    (0, 1),
)


def part_of(way, dist):
    return 0 if dist == 4 else 8 - 2 * dist + way


def kernel(
    q_hbm, c_hbm, gain_hbm, win_hbm, wout_hbm, proj_hbm, pos_hbm, asked_hbm, row_hbm, dest_hbm,
    loss_ref, grad_ref, index_ref,
    x, win, wout, proj, woutp, normed, hidden, cpart, qpart, base, crecv, qrecv,
    gain, pos, asked, row_of, dest, idx, codes, column, onehots, packed, embc, embq, sumq,
    fetch, cands, qall, slots, pieces, pieces_in, sums, sums_in, draw, draws, gshare, gshare_in,
    load_sem, c_s, c_r, qp_s, qp_r, code_s, code_r, col_s, col_r, plane_s, plane_r,
    fetch_s, fetch_r, q_s, q_r, piece_s, piece_r, idx_s, idx_r, sums_s, sums_r, draw_s, draw_r, grad_s, grad_r,
):
    g, d, z = lax.axis_index("group"), lax.axis_index("dp"), lax.axis_index("mp")
    y, xx = d // 4, lax.rem(d, 4)
    here = g * 16 + d
    right, left = lax.rem(z + 1, 8), lax.rem(z + 7, 8)

    def up(s):
        return lax.rem(z + s, 8)

    def across(dy, dx):
        return lax.rem(y + dy, 4) * 4 + lax.rem(xx + dx, 4)

    def owner(o):
        return {"group": o // 16, "dp": lax.rem(o, 16)}

    def remote(src, dst, send, recv, target):
        return pltpu.make_async_remote_copy(
            src_ref=src, dst_ref=dst, send_sem=send, recv_sem=recv, device_id=target, device_id_type=MESH)

    def home_of(i):
        even = (8 - i) // 2
        odd = 8 - (9 - i) // 2
        return lax.rem(z + jnp.where(lax.rem(i, 2) == 0, even, odd), 8)

    def load_x(i):
        rows = pl.ds(pl.multiple_of(home_of(jnp.int32(i)) * 256, 256), 256)
        return pltpu.make_async_copy(c_hbm.at[rows], x.at[i], load_sem.at[i])

    load_q = pltpu.make_async_copy(q_hbm, x.at[1], load_sem.at[1])
    load_in = pltpu.make_async_copy(win_hbm, win, load_sem.at[9])
    load_out = pltpu.make_async_copy(wout_hbm, wout, load_sem.at[10])
    load_proj = pltpu.make_async_copy(proj_hbm, proj, load_sem.at[11])
    load_small = [
        pltpu.make_async_copy(src, dst, load_sem.at[12 + k])
        for k, (src, dst) in enumerate((
            (gain_hbm, gain), (asked_hbm, asked), (row_hbm, row_of), (dest_hbm, dest), (pos_hbm, pos)))
    ]
    load_x(0).start()
    load_small[0].start()
    load_out.start()
    load_proj.start()
    load_in.start()
    load_q.start()
    for i in range(2, 9):
        load_x(i).start()

    for load in load_small[1:]:
        load.start()

    barrier = pltpu.get_barrier_semaphore()

    @pl.loop(1, 32)
    def _(s):
        pl.semaphore_signal(barrier, inc=1, device_id=owner(lax.rem(here + s, 32)), device_id_type=MESH)

    @pl.loop(1, 8)
    def _(s):
        pl.semaphore_signal(barrier, inc=1, device_id={"mp": up(s)}, device_id_type=MESH)

    def code_copy(to, frm):
        return remote(codes.at[d, frm], codes.at[d, frm], code_s.at[to], code_r.at[frm], {"mp": to})

    def column_copy(to, frm):
        return remote(column.at[frm], column.at[frm], col_s.at[to], col_r.at[frm], {"mp": to})

    def plane_copy(to, frm):
        return remote(codes.at[frm], codes.at[frm], plane_s.at[to], plane_r.at[frm], {"dp": to})

    def q_copy(to, frm):
        return remote(embq, qall.at[frm], q_s.at[to], q_r.at[frm], {"mp": to})

    def fetch_copy(pair, to, frm):
        return remote(
            fetch.at[pair, to], cands.at[pair, frm], fetch_s.at[pair, to], fetch_r.at[pair, frm], {"dp": to})

    def piece_copy(to, frm):
        return remote(pieces.at[to // 2], pieces_in.at[frm], piece_s.at[to], piece_r.at[frm], {"mp": to})

    def index_copy(to, frm):
        return remote(slots.at[to], index_ref.at[frm], idx_s.at[to], idx_r.at[frm], owner(to))

    def sums_copy(to, frm):
        return remote(sums.at[to], sums_in.at[frm], sums_s.at[to], sums_r.at[frm], {"mp": to})

    def draw_copy(to, frm):
        return remote(draw, draws.at[frm], draw_s.at[to], draw_r.at[frm], {"mp": to})

    def grad_copy(to, frm):
        return remote(gshare.at[to], gshare_in.at[frm], grad_s.at[to], grad_r.at[frm], owner(to))

    def spot(way, u):
        if u == 0:
            dist, half = 4, way
        elif u % 2 == 1:
            dist, half = 4 - (u + 1) // 2, 1 - way
        else:
            dist, half = 4 - u // 2, way
        return part_of(way, dist), slice(half * 128, half * 128 + 128), slice(half * 16, half * 16 + 16)

    def c_copy(way, u):
        i, rows, _ = spot(way, u)
        return remote(
            cpart.at[i, rows], crecv.at[way, u], c_s.at[way, u], c_r.at[way, u],
            {"mp": right if way == 0 else left})

    def qp_copy(way, u):
        i, _, rows = spot(way, u)
        return remote(
            qpart.at[i, rows], qrecv.at[way, u], qp_s.at[way, u], qp_r.at[way, u],
            {"mp": right if way == 0 else left})

    def q_unit(way, u):
        i, _, rows = spot(way, u)
        if u >= 2:
            qp_copy(way, u - 2).wait_recv()
            qpart[i, rows] = (qpart[i, rows].astype(f32) + qrecv[way, u - 2].astype(f32)).astype(bf16)
        qp_copy(way, u).start()

    def c_unit(way, u):
        i, rows, _ = spot(way, u)
        if u >= 2:
            c_copy(way, u - 2).wait_recv()
            cpart[i, rows] = (cpart[i, rows].astype(f32) + crecv[way, u - 2].astype(f32)).astype(bf16)
        c_copy(way, u).start()

    def both_units(u):
        q_unit(0, u)
        q_unit(1, u)
        c_unit(0, u)
        c_unit(1, u)

    def normalise(i, slot):
        for r in range(0, 256, 32):
            v = x[i, r:r + 32, :].astype(f32)
            scale = lax.rsqrt(jnp.mean(v * v, axis=-1, keepdims=True) + norm_eps)
            normed[slot, r:r + 32, :] = (v * scale * gain[...]).astype(bf16)

    def index_places():
        for load in load_small[1:]:
            load.wait()
        sub = lax.broadcasted_iota(jnp.int32, (256, 256), 0)
        lane = lax.broadcasted_iota(jnp.int32, (256, 256), 1)
        spread = jnp.where((lane[0:32] & 31) == sub[0:32], 1.0, 0.0).astype(bf16)
        of_row = (lane[0:8] >> 5) == sub[0:8]

        def flat(block):
            wide = jnp.dot(block.astype(f32).astype(bf16), spread, preferred_element_type=f32)
            return jnp.sum(jnp.where(of_row, wide, 0.0), axis=0, keepdims=True)

        def rank(row, earlier):
            column_form = jnp.sum(jnp.where(lane == sub, row, 0.0), axis=1, keepdims=True)
            return jnp.sum(jnp.where((column_form == row) & earlier, 1.0, 0.0), axis=0, keepdims=True)

        owners = flat(asked[...])
        slot = owners * 8.0 + rank(owners, (sub & 31) < (lane & 31))
        code = (slot * 256.0 + flat(row_of[...])).astype(jnp.int32)
        codes[d, z] = code
        mine = jnp.zeros((32, 128), jnp.int32)
        for k in range(8):
            of_k = jnp.sum(jnp.where(lane[0:32] - k * 32 == sub[0:32], code, 0), axis=1, keepdims=True)
            mine = jnp.where(lane[0:32, 0:128] == k, of_k, mine)
        column[z] = mine
        goal = dest[...].astype(f32)
        idx[...] = (goal * 16.0 + rank(goal, sub < lane)).astype(jnp.int32)

    load_x(0).wait()
    load_small[0].wait()
    load_out.wait()
    load_proj.wait()
    normalise(0, 0)
    woutp[...] = jnp.dot(wout[...], proj[...], preferred_element_type=f32).astype(bf16)
    load_in.wait()

    @pl.loop(0, 9)
    def _(i):
        @pl.when(i == 0)
        def _():
            load_q.wait()

        @pl.when(jnp.logical_and(i > 0, i < 8))
        def _():
            load_x(i + 1).wait()

        slot = lax.rem(i, 2)
        for n in range(2):
            rows = normed[slot]
            gate = jnp.dot(rows, win[:, n * 256:(n + 1) * 256], preferred_element_type=f32)
            upper = jnp.dot(rows, win[:, 512 + n * 256:768 + n * 256], preferred_element_type=f32)
            hidden[:, n * 256:(n + 1) * 256] = (gate / (1.0 + jnp.exp(-gate)) * upper).astype(bf16)
        normalise(jnp.minimum(i + 1, 8), 1 - slot)

        @pl.when(i == 0)
        def _():
            pl.semaphore_wait(barrier, 38)

        @pl.when(i == 1)
        def _():
            normed[1] = jnp.dot(hidden[...], wout[...], preferred_element_type=f32).astype(bf16)
            for k in (0, 2, 3, 4, 5, 6, 7, 8):
                h = home_of(jnp.int32(k))
                qpart[k] = normed[1, pl.ds(pl.multiple_of(h * 32, 32), 32), :]
            q_unit(0, 0)
            q_unit(1, 0)
            index_places()

            @pl.loop(1, 8)
            def _(s):
                code_copy(up(s), z).start()
                column_copy(up(s), z).start()

        @pl.when(i != 1)
        def _():
            cpart[i] = jnp.dot(hidden[...], woutp[...], preferred_element_type=f32).astype(bf16)

        @pl.when(i == 0)
        def _():
            c_unit(0, 0)
            c_unit(1, 0)

        @pl.when(i == 2)
        def _():
            q_unit(0, 1)
            c_unit(0, 1)

        @pl.when(i == 3)
        def _():
            q_unit(1, 1)
            c_unit(1, 1)

        @pl.when(i == 5)
        def _():
            both_units(2)

        @pl.when(i == 6)
        def _():
            @pl.loop(1, 8)
            def _(s):
                code_copy(z, up(s)).wait_recv()
                column_copy(z, up(s)).wait_recv()

            @pl.loop(1, 16)
            def _(s):
                plane_copy(lax.rem(d + s, 16), d).start()

    both_units(3)
    base[...] = jnp.dot(x[8], proj[...], preferred_element_type=f32) + cpart[8].astype(f32)

    @pl.loop(1, 16)
    def _(s):
        plane_copy(d, lax.rem(d + s, 16)).wait_recv()

    owner_slot = (d * 8 + z) * 8

    def wanted(pair):
        rank = lax.broadcasted_iota(jnp.int32, (8, 256), 0)
        lane = lax.broadcasted_iota(jnp.int32, (8, 256), 1)
        for c in range(16):
            for k in range(2):
                code = codes[c, pair * 2 + k]
                hit = (code >> 8) == owner_slot + rank
                row = jnp.sum(jnp.where(hit, (code & 255) + 1, 0), axis=1, keepdims=True) - 1
                packed[c * 16 + k * 8:c * 16 + k * 8 + 8, :] = jnp.where(lane == row, 1.0, 0.0)
        onehots[pair] = packed[...].astype(bf16)

    @pl.loop(0, 2)
    def _(pair):
        wanted(pair)

    both_units(4)

    @pl.loop(2, 4)
    def _(pair):
        wanted(pair)

    both_units(5)
    both_units(6)

    for way in (0, 1):
        for u in (5, 6):
            qp_copy(way, u).wait_recv()
    for half in range(2):
        rows = slice(half * 16, half * 16 + 16)
        own = x[1, pl.ds(pl.multiple_of(z * 32 + half * 16, 16), 16), :].astype(f32)
        mixed = (
            qpart[8, rows].astype(f32) + qrecv[0, 6 - half].astype(f32) + qrecv[1, 5 + half].astype(f32))
        sumq[rows, :] = (own + mixed).astype(bf16)
    raw = jnp.dot(sumq[...], proj[...], preferred_element_type=f32)
    length = jnp.sqrt(jnp.sum(raw * raw, axis=-1, keepdims=True) + embed_eps)
    unit = raw / length
    embq[...] = unit.astype(bf16)
    qall[z] = embq[...]
    for s in (6, 7, 5, 4, 3, 2, 1):
        q_copy(up(s), z).start()

    for way in (0, 1):
        for u in (5, 6):
            c_copy(way, u).wait_recv()
    for half in range(2):
        for r in range(0, 128, 64):
            rows = slice(half * 128 + r, half * 128 + r + 64)
            raw_c = (
                base[rows, :] + crecv[0, 6 - half, r:r + 64].astype(f32)
                + crecv[1, 5 + half, r:r + 64].astype(f32))
            inverse = lax.rsqrt(jnp.sum(raw_c * raw_c, axis=-1, keepdims=True) + embed_eps)
            embc[rows, :] = (raw_c * inverse).astype(bf16)

    def pair_at(s):
        return lax.rem(z // 2 + 1 + s, 4)

    @pl.loop(0, 4)
    def _(s):
        pair = pair_at(s)
        rows = jnp.dot(onehots[pair], embc[...], preferred_element_type=f32).astype(bf16)
        fetch[pair] = rows.reshape(16, 16, 768)
        for dy, dx in FAR_FIRST:
            fetch_copy(pair, across(dy, dx), d).start()
        cands[pair, d] = fetch[pair, d]

    turned = sumq[...].astype(f32).T.reshape(32, 4, 8, 32)
    for k in range(4):
        pieces[k] = turned[:, k].reshape(256, 32).T.astype(bf16)

    @pl.loop(1, 8)
    def _(s):
        piece_copy(up(s), z).start()

    pieces_in[z] = pieces[z // 2]

    @pl.loop(0, 2)
    def _(s):
        row = lax.broadcasted_iota(jnp.int32, (256, 256), 0) + s * 256
        onehot = jnp.where(row == idx[...], 1.0, 0.0).astype(bf16)
        rows = jnp.dot(onehot, embc[...], preferred_element_type=f32).astype(bf16)
        slots[pl.ds(s * 16, 16)] = rows.reshape(16, 16, 768)

    diagonal = lax.broadcasted_iota(jnp.int32, (32, 32), 0) == lax.broadcasted_iota(jnp.int32, (32, 32), 1)
    pos_column = jnp.sum(jnp.where(diagonal, pos[...], 0), axis=1, keepdims=True)
    at_pos = lax.broadcasted_iota(jnp.int32, (32, 256), 1) == pos_column
    positive = jnp.dot(jnp.where(at_pos, 1.0, 0.0).astype(bf16), embc[...], preferred_element_type=f32)
    pos_score = score_scale * jnp.sum(embq[...].astype(f32) * positive, axis=1, keepdims=True)
    pos_weight = jnp.exp(pos_score)

    @pl.loop(0, 4)
    def _(s):
        pair = pair_at(s)
        for k in range(2):
            @pl.when(pair * 2 + k != z)
            def _():
                q_copy(z, pair * 2 + k).wait_recv()

        @pl.loop(1, 16)
        def _(t):
            fetch_copy(pair, d, lax.rem(d + t, 16)).wait_recv()

        q = qall[pl.ds(pair * 2, 2)].reshape(64, 768)
        cand = cands[pair].reshape(256, 768)
        score = score_scale * lax.dot_general(
            q, cand, (((1,), (1,)), ((), ())), preferred_element_type=f32)
        row = lax.broadcasted_iota(jnp.int32, (64, 256), 0)
        lane = lax.broadcasted_iota(jnp.int32, (64, 256), 1)
        slot = ((lane >> 4) * 8 + z) * 8 + (lane & 7)
        wants = column[pl.ds(pair * 2, 2)].reshape(64, 128)
        hit = (wants[:, 0:1] >> 8) == slot
        for k in range(1, 8):
            hit = hit | ((wants[:, k:k + 1] >> 8) == slot)
        hit = hit & ((row >> 5) == ((lane >> 3) & 1))
        weight = jnp.where(hit, jnp.exp(score), 0.0)
        total = jnp.sum(weight, axis=1, keepdims=True)
        summed = jnp.dot(weight.astype(bf16), cand, preferred_element_type=f32).astype(bf16)
        high = total.astype(bf16).astype(f32)
        first = lax.broadcasted_iota(jnp.int32, (64, 128), 1) < 64
        tail = jnp.where(first, high, total - high).astype(bf16)
        for k in range(2):
            sums[pair * 2 + k, :, 0:768] = summed[k * 32:(k + 1) * 32]
            sums[pair * 2 + k, :, 768:896] = tail[k * 32:(k + 1) * 32]

            @pl.when(pair * 2 + k != z)
            def _():
                sums_copy(pair * 2 + k, z).start()

    sums_in[z] = sums[z]
    own_index = pltpu.make_async_copy(slots.at[here], index_ref.at[here], idx_s.at[here])
    own_index.start()
    for dy, dx in FAR_FIRST:
        for k in range(2):
            index_copy(k * 16 + across(dy, dx), here).start()
    index_copy((1 - g) * 16 + d, here).start()

    @pl.loop(1, 8)
    def _(s):
        sums_copy(z, up(s)).wait_recv()

    gathered = sums_in[0].astype(f32)
    for m in range(1, 8):
        gathered = gathered + sums_in[m].astype(f32)
    total = gathered[:, 768:769] + gathered[:, 832:833] + pos_weight
    loss = jnp.log(total) - pos_score
    loss_ref[...] = jnp.sum(jnp.where(diagonal, loss, 0.0), axis=0, keepdims=True)
    dunit = score_scale * ((gathered[:, 0:768] + pos_weight * positive) / total - positive)
    along = jnp.sum(unit * dunit, axis=1, keepdims=True)
    draw[...] = ((dunit - unit * along) / length).astype(bf16)
    for s in (4, 3, 5, 2, 6, 1, 7):
        draw_copy(up(s), z).start()
    draws[z] = draw[...]

    @pl.loop(1, 8)
    def _(s):
        piece_copy(z, up(s)).wait_recv()

    @pl.loop(1, 8)
    def _(s):
        draw_copy(z, up(s)).wait_recv()

    term = lax.dot_general(
        pieces_in[...].reshape(256, 256), draws[...].reshape(256, 768), (((0,), (0,)), ((), ())),
        preferred_element_type=f32).reshape(32, 8, 768)
    turned_term = jnp.concatenate([term[:, 4:8], term[:, 0:4]], axis=1)
    even = lax.rem(z, 2) == 0
    upper_rows = lax.broadcasted_iota(jnp.int32, (32, 8, 384), 1) < 4
    gshare[...] = jnp.where(
        upper_rows,
        jnp.where(even, term[:, :, 0:384], turned_term[:, :, 0:384]),
        jnp.where(even, turned_term[:, :, 384:768], term[:, :, 384:768]))
    for dy, dx in FAR_FIRST:
        for k in range(2):
            grad_copy(k * 16 + across(dy, dx), here).start()
    grad_copy((1 - g) * 16 + d, here).start()
    gshare_in[here] = gshare[here]

    for way in (0, 1):
        for u in range(7):
            qp_copy(way, u).wait_send()
            c_copy(way, u).wait_send()

    @pl.loop(1, 8)
    def _(s):
        code_copy(up(s), z).wait_send()
        column_copy(up(s), z).wait_send()
        q_copy(up(s), z).wait_send()
        piece_copy(up(s), z).wait_send()
        sums_copy(up(s), z).wait_send()
        draw_copy(up(s), z).wait_send()

    @pl.loop(1, 16)
    def _(s):
        to = lax.rem(d + s, 16)
        plane_copy(to, d).wait_send()
        for pair in range(4):
            fetch_copy(pair, to, d).wait_send()

    own_index.wait()

    @pl.loop(1, 32)
    def _(s):
        other = lax.rem(here + s, 32)
        index_copy(other, here).wait_send()
        index_copy(here, other).wait_recv()

    @pl.loop(1, 32)
    def _(s):
        other = lax.rem(here + s, 32)
        grad_copy(other, here).wait_send()
        grad_copy(here, other).wait_recv()

    grad = jnp.sum(gshare_in[...], axis=0)
    grad_ref[:, 0:384] = grad[0:4]
    grad_ref[:, 384:768] = grad[4:8]


def fused(*args):
    hbm = pl.BlockSpec(memory_space=pl.ANY)
    vmem = pl.BlockSpec(memory_space=pltpu.VMEM)
    sds = jax.ShapeDtypeStruct
    dma = pltpu.SemaphoreType.DMA
    return pl.pallas_call(
        kernel,
        out_shape=(sds((1, 32), f32), sds((4, 768), f32), sds((32, 16, 768), bf16)),
        in_specs=[hbm] * 10,
        out_specs=[vmem, vmem, hbm],
        scratch_shapes=[
            pltpu.VMEM((9, 256, 1024), bf16),
            pltpu.VMEM((1024, 1024), bf16),
            pltpu.VMEM((512, 1024), bf16),
            pltpu.VMEM((1024, 768), bf16),
            pltpu.VMEM((512, 768), bf16),
            pltpu.VMEM((2, 256, 1024), bf16),
            pltpu.VMEM((256, 512), bf16),
            pltpu.VMEM((9, 256, 768), bf16),
            pltpu.VMEM((9, 32, 1024), bf16),
            pltpu.VMEM((256, 768), f32),
            pltpu.VMEM((2, 7, 128, 768), bf16),
            pltpu.VMEM((2, 7, 16, 1024), bf16),
            pltpu.VMEM((1, 1024), f32),
            pltpu.VMEM((1, 32), jnp.int32),
            pltpu.VMEM((8, 32), jnp.int32),
            pltpu.VMEM((8, 32), jnp.int32),
            pltpu.VMEM((1, 256), jnp.int32),
            pltpu.VMEM((1, 256), jnp.int32),
            pltpu.VMEM((16, 8, 1, 256), jnp.int32),
            pltpu.VMEM((8, 32, 128), jnp.int32),
            pltpu.VMEM((4, 256, 256), bf16),
            pltpu.VMEM((256, 256), f32),
            pltpu.VMEM((256, 768), bf16),
            pltpu.VMEM((32, 768), bf16),
            pltpu.VMEM((32, 1024), bf16),
            pltpu.VMEM((4, 16, 16, 768), bf16),
            pltpu.VMEM((4, 16, 16, 768), bf16),
            pltpu.VMEM((8, 32, 768), bf16),
            pltpu.VMEM((32, 16, 768), bf16),
            pltpu.VMEM((4, 32, 256), bf16),
            pltpu.VMEM((8, 32, 256), bf16),
            pltpu.VMEM((8, 32, 896), bf16),
            pltpu.VMEM((8, 32, 896), bf16),
            pltpu.VMEM((32, 768), bf16),
            pltpu.VMEM((8, 32, 768), bf16),
            pltpu.VMEM((32, 8, 384), f32),
            pltpu.VMEM((32, 8, 384), f32),
            dma((17,)), dma((2, 7)), dma((2, 7)), dma((2, 7)), dma((2, 7)), dma((8,)), dma((8,)), dma((8,)), dma((8,)),
            dma((16,)), dma((16,)), dma((4, 16)), dma((4, 16)), dma((8,)), dma((8,)), dma((8,)), dma((8,)),
            dma((32,)), dma((32,)), dma((8,)), dma((8,)), dma((8,)), dma((8,)), dma((32,)), dma((32,)),
        ],
        compiler_params=pltpu.CompilerParams(
            collective_id=0, has_side_effects=True, vmem_limit_bytes=52 * 1024 * 1024),
        cost_estimate=pl.CostEstimate(flops=11_000_000_000, bytes_accessed=20_000_000, transcendentals=2_000_000),
        name="fused",
    )(*args)


def per_device(
    queries, clips, norm_gain, w_in, w_out, proj, pos_row, neg_owner, neg_row, clip_dest
):
    width = queries.shape[1]
    loss, grad, index = fused(
        queries, clips, norm_gain.reshape(1, width), w_in.reshape(width, -1), w_out, proj,
        pos_row.reshape(1, -1), neg_owner.T, neg_row.T, clip_dest.reshape(1, -1))
    return (loss.reshape(-1), index.reshape(-1, index.shape[-1]), grad)


def solution(mesh):
    return jax.shard_map(
        per_device,
        mesh=mesh,
        in_specs=(
            P(("group", "dp"), None),
            P(("group", "dp"), None),
            P(),
            P(None, None, "mp"),
            P("mp", None),
            P(),
            P(("group", "dp", "mp")),
            P(("group", "dp", "mp"), None),
            P(("group", "dp", "mp"), None),
            P(("group", "dp", "mp"), None),
        ),
        out_specs=(
            P(("group", "dp", "mp")),
            P(("group", "dp", "mp"), None),
            P(("group", "dp", "mp"), None),
        ),
        check_vma=False,
    )
```

```python
import jax
import jax.numpy as jnp
from jax import lax
from jax.experimental import pallas as pl
from jax.experimental.pallas import tpu as pltpu
from jax.sharding import PartitionSpec as P

norm_eps = 1e-06
embed_eps = 1e-06
score_scale = 20.0
MESH = pl.DeviceIdType.MESH
f32 = jnp.float32
bf16 = jnp.bfloat16
FAR_FIRST = (
    (2, 2), (3, 2), (2, 3), (2, 1), (1, 2), (3, 1), (1, 3), (3, 3), (1, 1), (0, 2), (2, 0), (3, 0), (0, 3), (1, 0),
    (0, 1),
)


def part_of(way, dist):
    return 0 if dist == 4 else 8 - 2 * dist + way


def kernel(
    q_hbm, c_hbm, gain_hbm, win_hbm, wout_hbm, proj_hbm, pos_hbm, asked_hbm, row_hbm, dest_hbm,
    loss_ref, grad_ref, index_ref,
    x, win, wout, proj, woutp, normed, hidden, cpart, qpart, base, crecv, qrecv,
    gain, pos, asked, row_of, dest, idx, codes, column, onehots, packed, embc, embq, sumq,
    fetch, cands, qall, slots, pieces, pieces_in, sums, sums_in, draw, draws, gshare, gshare_in,
    load_sem, c_s, c_r, qp_s, qp_r, q_r, fetch_s, fetch_r,
    code_s, code_r, plane_s, plane_r, q_s, piece_s, piece_r, own_s, idx_s, idx_r, sums_s, sums_r, draw_s, draw_r,
    grad_s, grad_r,
):
    g, d, z = lax.axis_index("group"), lax.axis_index("dp"), lax.axis_index("mp")
    y, xx = d // 4, lax.rem(d, 4)
    here = g * 16 + d
    right, left = lax.rem(z + 1, 8), lax.rem(z + 7, 8)

    def up(s):
        return lax.rem(z + s, 8)

    def across(dy, dx):
        return lax.rem(y + dy, 4) * 4 + lax.rem(xx + dx, 4)

    def owner(o):
        return {"group": o // 16, "dp": lax.rem(o, 16)}

    def remote(src, dst, send, recv, target):
        return pltpu.make_async_remote_copy(
            src_ref=src, dst_ref=dst, send_sem=send, recv_sem=recv, device_id=target, device_id_type=MESH)

    def home_of(i):
        even = (8 - i) // 2
        odd = 8 - (9 - i) // 2
        return lax.rem(z + jnp.where(lax.rem(i, 2) == 0, even, odd), 8)

    def load_x(i):
        rows = pl.ds(pl.multiple_of(home_of(jnp.int32(i)) * 256, 256), 256)
        return pltpu.make_async_copy(c_hbm.at[rows], x.at[i], load_sem.at[i])

    load_q = pltpu.make_async_copy(q_hbm, x.at[1], load_sem.at[1])
    load_in = pltpu.make_async_copy(win_hbm, win, load_sem.at[9])
    load_out = pltpu.make_async_copy(wout_hbm, wout, load_sem.at[10])
    load_proj = pltpu.make_async_copy(proj_hbm, proj, load_sem.at[11])
    load_small = [
        pltpu.make_async_copy(src, dst, load_sem.at[12 + k])
        for k, (src, dst) in enumerate((
            (gain_hbm, gain), (asked_hbm, asked), (row_hbm, row_of), (dest_hbm, dest), (pos_hbm, pos)))
    ]
    load_x(0).start()
    load_small[0].start()
    load_out.start()
    load_proj.start()
    load_in.start()
    load_q.start()
    for i in range(2, 9):
        load_x(i).start()

    for load in load_small[1:]:
        load.start()

    barrier = pltpu.get_barrier_semaphore()

    @pl.loop(1, 32)
    def _(s):
        pl.semaphore_signal(barrier, inc=1, device_id=owner(lax.rem(here + s, 32)), device_id_type=MESH)

    @pl.loop(1, 8)
    def _(s):
        pl.semaphore_signal(barrier, inc=1, device_id={"mp": up(s)}, device_id_type=MESH)

    def code_copy(to, frm):
        return remote(codes.at[d, frm], codes.at[d, frm], code_s, code_r, {"mp": to})

    def plane_copy(to, frm):
        return remote(codes.at[frm], codes.at[frm], plane_s, plane_r, {"dp": to})

    def q_copy(to, frm):
        return remote(embq, qall.at[frm], q_s, q_r.at[frm], {"mp": to})

    def fetch_copy(pair, to, frm):
        return remote(fetch.at[pair, to], cands.at[pair, frm], fetch_s.at[pair], fetch_r.at[pair], {"dp": to})

    def piece_copy(to, frm):
        return remote(pieces.at[to // 2], pieces_in.at[frm], piece_s, piece_r, {"mp": to})

    def index_copy(to, frm):
        return remote(slots.at[to], index_ref.at[frm], idx_s, idx_r, owner(to))

    def sums_copy(to, frm):
        return remote(sums.at[to], sums_in.at[frm], sums_s, sums_r, {"mp": to})

    def draw_copy(to, frm):
        return remote(draw, draws.at[frm], draw_s, draw_r, {"mp": to})

    def grad_copy(to, frm):
        return remote(gshare.at[to], gshare_in.at[frm], grad_s, grad_r, owner(to))

    def wait_batch(ref, semaphore):
        pltpu.make_async_copy(ref, ref, semaphore).wait()

    def spot(way, u):
        if u == 0:
            dist, half = 4, way
        elif u % 2 == 1:
            dist, half = 4 - (u + 1) // 2, 1 - way
        else:
            dist, half = 4 - u // 2, way
        return part_of(way, dist), half

    def c_copy(way, n):
        i, half = spot(way, n // 2)
        start = half * 128 + n % 2 * 64
        return remote(
            cpart.at[i, start:start + 64], crecv.at[way, n], c_s.at[way, n % 2], c_r.at[way, n],
            {"mp": right if way == 0 else left})

    def qp_copy(way, u):
        i, half = spot(way, u)
        return remote(
            qpart.at[i, half * 16:half * 16 + 16], qrecv.at[way, u], qp_s.at[way, u % 2], qp_r.at[way, u],
            {"mp": right if way == 0 else left})

    def q_unit(way, u):
        i, half = spot(way, u)
        rows = slice(half * 16, half * 16 + 16)
        if u >= 2:
            qp_copy(way, u - 2).wait_recv()
            qpart[i, rows] = (qpart[i, rows].astype(f32) + qrecv[way, u - 2].astype(f32)).astype(bf16)
            qp_copy(way, u - 2).wait_send()
        qp_copy(way, u).start()

    def c_unit(way, n):
        i, half = spot(way, n // 2)
        rows = slice(half * 128 + n % 2 * 64, half * 128 + n % 2 * 64 + 64)
        if n >= 4:
            c_copy(way, n - 4).wait_recv()
            cpart[i, rows] = (cpart[i, rows].astype(f32) + crecv[way, n - 4].astype(f32)).astype(bf16)
        if n >= 2:
            c_copy(way, n - 2).wait_send()
        c_copy(way, n).start()

    def c_units(u):
        for n in (2 * u, 2 * u + 1):
            c_unit(0, n)
            c_unit(1, n)

    def both_units(u):
        q_unit(0, u)
        q_unit(1, u)
        c_units(u)

    def normalise(i, slot):
        for r in range(0, 256, 32):
            v = x[i, r:r + 32, :].astype(f32)
            scale = lax.rsqrt(jnp.mean(v * v, axis=-1, keepdims=True) + norm_eps)
            normed[slot, r:r + 32, :] = (v * scale * gain[...]).astype(bf16)

    def index_places():
        for load in load_small[1:]:
            load.wait()
        sub = lax.broadcasted_iota(jnp.int32, (256, 256), 0)
        lane = lax.broadcasted_iota(jnp.int32, (256, 256), 1)
        spread = jnp.where((lane[0:32] & 31) == sub[0:32], 1.0, 0.0).astype(bf16)
        of_row = (lane[0:8] >> 5) == sub[0:8]

        def flat(block):
            wide = jnp.dot(block.astype(f32).astype(bf16), spread, preferred_element_type=f32)
            return jnp.sum(jnp.where(of_row, wide, 0.0), axis=0, keepdims=True)

        def rank(row, earlier):
            column_form = jnp.sum(jnp.where(lane == sub, row, 0.0), axis=1, keepdims=True)
            return jnp.sum(jnp.where((column_form == row) & earlier, 1.0, 0.0), axis=0, keepdims=True)

        owners = flat(asked[...])
        slot = owners * 8.0 + rank(owners, (sub & 31) < (lane & 31))
        code = (slot * 256.0 + flat(row_of[...])).astype(jnp.int32)
        codes[d, z] = code
        goal = dest[...].astype(f32)
        idx[...] = (goal * 16.0 + rank(goal, sub < lane)).astype(jnp.int32)

    load_x(0).wait()
    load_small[0].wait()
    load_out.wait()
    load_proj.wait()
    normalise(0, 0)
    woutp[...] = jnp.dot(wout[...], proj[...], preferred_element_type=f32).astype(bf16)
    load_in.wait()

    @pl.loop(0, 9)
    def _(i):
        @pl.when(i == 0)
        def _():
            load_q.wait()

        @pl.when(jnp.logical_and(i > 0, i < 8))
        def _():
            load_x(i + 1).wait()

        slot = lax.rem(i, 2)
        for n in range(2):
            rows = normed[slot]
            gate = jnp.dot(rows, win[:, n * 256:(n + 1) * 256], preferred_element_type=f32)
            upper = jnp.dot(rows, win[:, 512 + n * 256:768 + n * 256], preferred_element_type=f32)
            hidden[:, n * 256:(n + 1) * 256] = (gate / (1.0 + jnp.exp(-gate)) * upper).astype(bf16)
        normalise(jnp.minimum(i + 1, 8), 1 - slot)

        @pl.when(i == 0)
        def _():
            pl.semaphore_wait(barrier, 38)

        @pl.when(i == 1)
        def _():
            normed[1] = jnp.dot(hidden[...], wout[...], preferred_element_type=f32).astype(bf16)
            for k in (0, 2, 3, 4, 5, 6, 7, 8):
                h = home_of(jnp.int32(k))
                qpart[k] = normed[1, pl.ds(pl.multiple_of(h * 32, 32), 32), :]
            q_unit(0, 0)
            q_unit(1, 0)
            index_places()

            @pl.loop(1, 8)
            def _(s):
                code_copy(up(s), z).start()

        @pl.when(i != 1)
        def _():
            cpart[i] = jnp.dot(hidden[...], woutp[...], preferred_element_type=f32).astype(bf16)

        @pl.when(i == 0)
        def _():
            c_units(0)

        @pl.when(i == 3)
        def _():
            both_units(1)

        @pl.when(i == 5)
        def _():
            both_units(2)

        @pl.when(i == 6)
        def _():
            wait_batch(codes.at[d, 0:7], code_r)

            @pl.loop(1, 16)
            def _(s):
                plane_copy(lax.rem(d + s, 16), d).start()

        @pl.when(i == 7)
        def _():
            both_units(3)

    base[...] = jnp.dot(x[8], proj[...], preferred_element_type=f32) + cpart[8].astype(f32)
    both_units(4)
    wait_batch(codes.at[0:15], plane_r)

    owner_slot = (d * 8 + z) * 8

    def wanted(pair):
        rank = lax.broadcasted_iota(jnp.int32, (8, 256), 0)
        lane = lax.broadcasted_iota(jnp.int32, (8, 256), 1)
        for c in range(16):
            for k in range(2):
                code = codes[c, pair * 2 + k]
                hit = (code >> 8) == owner_slot + rank
                row = jnp.sum(jnp.where(hit, (code & 255) + 1, 0), axis=1, keepdims=True) - 1
                packed[c * 16 + k * 8:c * 16 + k * 8 + 8, :] = jnp.where(lane == row, 1.0, 0.0)
        onehots[pair] = packed[...].astype(bf16)

    @pl.loop(0, 4)
    def _(pair):
        wanted(pair)

    both_units(5)

    @pl.loop(0, 8)
    def _(m):
        sub = lax.broadcasted_iota(jnp.int32, (32, 256), 0)
        lane = lax.broadcasted_iota(jnp.int32, (32, 256), 1)
        code = codes[d, m]
        wants = jnp.zeros((32, 128), jnp.int32)
        for k in range(8):
            of_k = jnp.sum(jnp.where(lane - k * 32 == sub, code, 0), axis=1, keepdims=True)
            wants = jnp.where(lane[:, 0:128] == k, of_k, wants)
        column[m] = wants

    both_units(6)

    for way in (0, 1):
        for u in (5, 6):
            qp_copy(way, u).wait_recv()
    for half in range(2):
        rows = slice(half * 16, half * 16 + 16)
        own = x[1, pl.ds(pl.multiple_of(z * 32 + half * 16, 16), 16), :].astype(f32)
        mixed = (
            qpart[8, rows].astype(f32) + qrecv[0, 6 - half].astype(f32) + qrecv[1, 5 + half].astype(f32))
        sumq[rows, :] = (own + mixed).astype(bf16)
    raw = jnp.dot(sumq[...], proj[...], preferred_element_type=f32)
    length = jnp.sqrt(jnp.sum(raw * raw, axis=-1, keepdims=True) + embed_eps)
    unit = raw / length
    embq[...] = unit.astype(bf16)
    qall[z] = embq[...]
    for s in (6, 7, 5, 4, 3, 2, 1):
        q_copy(up(s), z).start()

    for way in (0, 1):
        for n in (10, 11, 12, 13):
            c_copy(way, n).wait_recv()
    for half in range(2):
        for r in range(2):
            rows = slice(half * 128 + r * 64, half * 128 + r * 64 + 64)
            raw_c = (
                base[rows, :] + crecv[0, 12 - 2 * half + r].astype(f32) + crecv[1, 10 + 2 * half + r].astype(f32))
            inverse = lax.rsqrt(jnp.sum(raw_c * raw_c, axis=-1, keepdims=True) + embed_eps)
            embc[rows, :] = (raw_c * inverse).astype(bf16)

    def pair_at(s):
        return lax.rem(z // 2 + 1 + s, 4)

    def send_fetch(s):
        pair = pair_at(s)
        for dy, dx in FAR_FIRST:
            fetch_copy(pair, across(dy, dx), d).start()

    @pl.loop(0, 4)
    def _(s):
        pair = pair_at(s)
        rows = jnp.dot(onehots[pair], embc[...], preferred_element_type=f32).astype(bf16)
        fetch[pair] = rows.reshape(16, 16, 768)

        @pl.when(s == 0)
        def _():
            send_fetch(0)

        cands[pair, d] = fetch[pair, d]

    turned = sumq[...].astype(f32).T.reshape(32, 4, 8, 32)
    for k in range(4):
        pieces[k] = turned[:, k].reshape(256, 32).T.astype(bf16)

    @pl.loop(1, 8)
    def _(s):
        piece_copy(up(s), z).start()

    pieces_in[z] = pieces[z // 2]

    @pl.loop(0, 2)
    def _(s):
        row = lax.broadcasted_iota(jnp.int32, (256, 256), 0) + s * 256
        onehot = jnp.where(row == idx[...], 1.0, 0.0).astype(bf16)
        rows = jnp.dot(onehot, embc[...], preferred_element_type=f32).astype(bf16)
        slots[pl.ds(s * 16, 16)] = rows.reshape(16, 16, 768)

    diagonal = lax.broadcasted_iota(jnp.int32, (32, 32), 0) == lax.broadcasted_iota(jnp.int32, (32, 32), 1)
    pos_column = jnp.sum(jnp.where(diagonal, pos[...], 0), axis=1, keepdims=True)
    at_pos = lax.broadcasted_iota(jnp.int32, (32, 256), 1) == pos_column
    positive = jnp.dot(jnp.where(at_pos, 1.0, 0.0).astype(bf16), embc[...], preferred_element_type=f32)
    pos_score = score_scale * jnp.sum(embq[...].astype(f32) * positive, axis=1, keepdims=True)
    pos_weight = jnp.exp(pos_score)

    send_fetch(1)

    @pl.loop(0, 4)
    def _(s):
        pair = pair_at(s)
        wait_batch(cands.at[pair, 0:15], fetch_r.at[pair])
        wait_batch(fetch.at[pair, 0:15], fetch_s.at[pair])

        @pl.when(s < 2)
        def _():
            send_fetch(s + 2)

        for k in range(2):
            @pl.when(pair * 2 + k != z)
            def _():
                q_copy(z, pair * 2 + k).wait_recv()

        q = qall[pl.ds(pair * 2, 2)].reshape(64, 768)
        cand = cands[pair].reshape(256, 768)
        score = score_scale * lax.dot_general(
            q, cand, (((1,), (1,)), ((), ())), preferred_element_type=f32)
        row = lax.broadcasted_iota(jnp.int32, (64, 256), 0)
        lane = lax.broadcasted_iota(jnp.int32, (64, 256), 1)
        slot = ((lane >> 4) * 8 + z) * 8 + (lane & 7)
        wants = column[pl.ds(pair * 2, 2)].reshape(64, 128)
        hit = (wants[:, 0:1] >> 8) == slot
        for k in range(1, 8):
            hit = hit | ((wants[:, k:k + 1] >> 8) == slot)
        hit = hit & ((row >> 5) == ((lane >> 3) & 1))
        weight = jnp.where(hit, jnp.exp(score), 0.0)
        total = jnp.sum(weight, axis=1, keepdims=True)
        summed = jnp.dot(weight.astype(bf16), cand, preferred_element_type=f32).astype(bf16)
        high = total.astype(bf16).astype(f32)
        first = lax.broadcasted_iota(jnp.int32, (64, 128), 1) < 64
        tail = jnp.where(first, high, total - high).astype(bf16)
        for k in range(2):
            sums[pair * 2 + k, :, 0:768] = summed[k * 32:(k + 1) * 32]
            sums[pair * 2 + k, :, 768:896] = tail[k * 32:(k + 1) * 32]

            @pl.when(pair * 2 + k != z)
            def _():
                sums_copy(pair * 2 + k, z).start()

    sums_in[z] = sums[z]
    own_index = pltpu.make_async_copy(slots.at[here], index_ref.at[here], own_s)
    own_index.start()
    for dy, dx in FAR_FIRST:
        for k in range(2):
            index_copy(k * 16 + across(dy, dx), here).start()
    index_copy((1 - g) * 16 + d, here).start()

    wait_batch(sums_in.at[0:7], sums_r)

    gathered = sums_in[0].astype(f32)
    for m in range(1, 8):
        gathered = gathered + sums_in[m].astype(f32)
    total = gathered[:, 768:769] + gathered[:, 832:833] + pos_weight
    loss = jnp.log(total) - pos_score
    loss_ref[...] = jnp.sum(jnp.where(diagonal, loss, 0.0), axis=0, keepdims=True)
    dunit = score_scale * ((gathered[:, 0:768] + pos_weight * positive) / total - positive)
    along = jnp.sum(unit * dunit, axis=1, keepdims=True)
    draw[...] = ((dunit - unit * along) / length).astype(bf16)
    for s in (4, 3, 5, 2, 6, 1, 7):
        draw_copy(up(s), z).start()
    draws[z] = draw[...]

    wait_batch(pieces_in.at[0:7], piece_r)
    wait_batch(draws.at[0:7], draw_r)

    term = lax.dot_general(
        pieces_in[...].reshape(256, 256), draws[...].reshape(256, 768), (((0,), (0,)), ((), ())),
        preferred_element_type=f32).reshape(32, 8, 768)
    turned_term = jnp.concatenate([term[:, 4:8], term[:, 0:4]], axis=1)
    even = lax.rem(z, 2) == 0
    upper_rows = lax.broadcasted_iota(jnp.int32, (32, 8, 384), 1) < 4
    gshare[...] = jnp.where(
        upper_rows,
        jnp.where(even, term[:, :, 0:384], turned_term[:, :, 0:384]),
        jnp.where(even, turned_term[:, :, 384:768], term[:, :, 384:768]))
    for dy, dx in FAR_FIRST:
        for k in range(2):
            grad_copy(k * 16 + across(dy, dx), here).start()
    grad_copy((1 - g) * 16 + d, here).start()
    gshare_in[here] = gshare[here]

    for way in (0, 1):
        for u in (5, 6):
            qp_copy(way, u).wait_send()
        for n in (12, 13):
            c_copy(way, n).wait_send()
    wait_batch(codes.at[d, 0:7], code_s)
    wait_batch(codes.at[0:15], plane_s)
    wait_batch(qall.at[0:7], q_s)
    wait_batch(pieces_in.at[0:7], piece_s)
    wait_batch(sums.at[0:7], sums_s)
    wait_batch(draws.at[0:7], draw_s)
    own_index.wait()
    wait_batch(slots.at[0:31], idx_s)
    wait_batch(index_ref.at[0:31], idx_r)
    wait_batch(gshare.at[0:31], grad_s)
    wait_batch(gshare_in.at[0:31], grad_r)
    grad = jnp.sum(gshare_in[...], axis=0)
    grad_ref[:, 0:384] = grad[0:4]
    grad_ref[:, 384:768] = grad[4:8]


def fused(*args):
    hbm = pl.BlockSpec(memory_space=pl.ANY)
    vmem = pl.BlockSpec(memory_space=pltpu.VMEM)
    sds = jax.ShapeDtypeStruct
    dma = pltpu.SemaphoreType.DMA
    return pl.pallas_call(
        kernel,
        out_shape=(sds((1, 32), f32), sds((4, 768), f32), sds((32, 16, 768), bf16)),
        in_specs=[hbm] * 10,
        out_specs=[vmem, vmem, hbm],
        scratch_shapes=[
            pltpu.VMEM((9, 256, 1024), bf16),
            pltpu.VMEM((1024, 1024), bf16),
            pltpu.VMEM((512, 1024), bf16),
            pltpu.VMEM((1024, 768), bf16),
            pltpu.VMEM((512, 768), bf16),
            pltpu.VMEM((2, 256, 1024), bf16),
            pltpu.VMEM((256, 512), bf16),
            pltpu.VMEM((9, 256, 768), bf16),
            pltpu.VMEM((9, 32, 1024), bf16),
            pltpu.VMEM((256, 768), f32),
            pltpu.VMEM((2, 14, 64, 768), bf16),
            pltpu.VMEM((2, 7, 16, 1024), bf16),
            pltpu.VMEM((1, 1024), f32),
            pltpu.VMEM((1, 32), jnp.int32),
            pltpu.VMEM((8, 32), jnp.int32),
            pltpu.VMEM((8, 32), jnp.int32),
            pltpu.VMEM((1, 256), jnp.int32),
            pltpu.VMEM((1, 256), jnp.int32),
            pltpu.VMEM((16, 8, 1, 256), jnp.int32),
            pltpu.VMEM((8, 32, 128), jnp.int32),
            pltpu.VMEM((4, 256, 256), bf16),
            pltpu.VMEM((256, 256), f32),
            pltpu.VMEM((256, 768), bf16),
            pltpu.VMEM((32, 768), bf16),
            pltpu.VMEM((32, 1024), bf16),
            pltpu.VMEM((4, 16, 16, 768), bf16),
            pltpu.VMEM((4, 16, 16, 768), bf16),
            pltpu.VMEM((8, 32, 768), bf16),
            pltpu.VMEM((32, 16, 768), bf16),
            pltpu.VMEM((4, 32, 256), bf16),
            pltpu.VMEM((8, 32, 256), bf16),
            pltpu.VMEM((8, 32, 896), bf16),
            pltpu.VMEM((8, 32, 896), bf16),
            pltpu.VMEM((32, 768), bf16),
            pltpu.VMEM((8, 32, 768), bf16),
            pltpu.VMEM((32, 8, 384), f32),
            pltpu.VMEM((32, 8, 384), f32),
            dma((17,)), dma((2, 2)), dma((2, 14)), dma((2, 2)), dma((2, 7)), dma((8,)), dma((4,)), dma((4,)),
            *[dma] * 16,
        ],
        compiler_params=pltpu.CompilerParams(
            collective_id=0, has_side_effects=True, vmem_limit_bytes=52 * 1024 * 1024),
        cost_estimate=pl.CostEstimate(flops=11_000_000_000, bytes_accessed=20_000_000, transcendentals=2_000_000),
        name="fused",
    )(*args)


def per_device(
    queries, clips, norm_gain, w_in, w_out, proj, pos_row, neg_owner, neg_row, clip_dest
):
    width = queries.shape[1]
    loss, grad, index = fused(
        queries, clips, norm_gain.reshape(1, width), w_in.reshape(width, -1), w_out, proj,
        pos_row.reshape(1, -1), neg_owner.T, neg_row.T, clip_dest.reshape(1, -1))
    return (loss.reshape(-1), index.reshape(-1, index.shape[-1]), grad)


def solution(mesh):
    return jax.shard_map(
        per_device,
        mesh=mesh,
        in_specs=(
            P(("group", "dp"), None),
            P(("group", "dp"), None),
            P(),
            P(None, None, "mp"),
            P("mp", None),
            P(),
            P(("group", "dp", "mp")),
            P(("group", "dp", "mp"), None),
            P(("group", "dp", "mp"), None),
            P(("group", "dp", "mp"), None),
        ),
        out_specs=(
            P(("group", "dp", "mp")),
            P(("group", "dp", "mp"), None),
            P(("group", "dp", "mp"), None),
        ),
        check_vma=False,
    )
```

```python
import jax
import jax.numpy as jnp
from jax import lax
from jax.experimental import pallas as pl
from jax.experimental.pallas import tpu as pltpu
from jax.sharding import PartitionSpec as P

norm_eps = 1e-06
embed_eps = 1e-06
score_scale = 20.0
MESH = pl.DeviceIdType.MESH
f32 = jnp.float32
bf16 = jnp.bfloat16
FAR_FIRST = (
    (2, 2), (3, 2), (2, 3), (2, 1), (1, 2), (3, 1), (1, 3), (3, 3), (1, 1), (0, 2), (2, 0), (3, 0), (0, 3), (1, 0),
    (0, 1),
)


def part_of(way, dist):
    return 0 if dist == 4 else 8 - 2 * dist + way


def kernel(
    q_hbm, c_hbm, gain_hbm, win_hbm, wout_hbm, proj_hbm, pos_hbm, asked_hbm, row_hbm, dest_hbm,
    loss_ref, grad_ref, index_ref,
    x, win, wout, proj, woutp, normed, hidden, cpart, qpart, base, crecv, qrecv,
    gain, pos, asked, row_of, dest, idx, codes, column, onehots, packed, embc, embq, sumq,
    fetch, cands, qall, slots, pieces, pieces_in, turned_in, sums, sums_in, draw, draws, gshare, gshare_in, gpart,
    load_sem, c_s, c_r, qp_s, qp_r, q_r, fetch_s, fetch_r,
    code_s, code_r, plane_s, plane_r, q_s, piece_s, piece_r, own_s, idx_s, idx_r, sums_s, sums_r, draw_s, draw_r,
    grad_s, grad_r, part_s, part_r,
):
    g, d, z = lax.axis_index("group"), lax.axis_index("dp"), lax.axis_index("mp")
    y, xx = d // 4, lax.rem(d, 4)
    here = g * 16 + d
    right, left = lax.rem(z + 1, 8), lax.rem(z + 7, 8)

    def up(s):
        return lax.rem(z + s, 8)

    def across(dy, dx):
        return lax.rem(y + dy, 4) * 4 + lax.rem(xx + dx, 4)

    def owner(o):
        return {"group": o // 16, "dp": lax.rem(o, 16)}

    def remote(src, dst, send, recv, target):
        return pltpu.make_async_remote_copy(
            src_ref=src, dst_ref=dst, send_sem=send, recv_sem=recv, device_id=target, device_id_type=MESH)

    def home_of(i):
        even = (8 - i) // 2
        odd = 8 - (9 - i) // 2
        return lax.rem(z + jnp.where(lax.rem(i, 2) == 0, even, odd), 8)

    def load_x(i):
        rows = pl.ds(pl.multiple_of(home_of(jnp.int32(i)) * 256, 256), 256)
        return pltpu.make_async_copy(c_hbm.at[rows], x.at[i], load_sem.at[i])

    load_q = pltpu.make_async_copy(q_hbm, x.at[1], load_sem.at[1])
    load_in = pltpu.make_async_copy(win_hbm, win, load_sem.at[9])
    load_out = pltpu.make_async_copy(wout_hbm, wout, load_sem.at[10])
    load_proj = pltpu.make_async_copy(proj_hbm, proj, load_sem.at[11])
    load_small = [
        pltpu.make_async_copy(src, dst, load_sem.at[12 + k])
        for k, (src, dst) in enumerate((
            (gain_hbm, gain), (asked_hbm, asked), (row_hbm, row_of), (dest_hbm, dest), (pos_hbm, pos)))
    ]
    load_x(0).start()
    load_small[0].start()
    load_out.start()
    load_proj.start()
    load_in.start()
    load_q.start()
    for i in range(2, 9):
        load_x(i).start()

    for load in load_small[1:]:
        load.start()

    barrier = pltpu.get_barrier_semaphore()

    @pl.loop(1, 32)
    def _(s):
        pl.semaphore_signal(barrier, inc=1, device_id=owner(lax.rem(here + s, 32)), device_id_type=MESH)

    @pl.loop(1, 8)
    def _(s):
        pl.semaphore_signal(barrier, inc=1, device_id={"mp": up(s)}, device_id_type=MESH)

    def code_copy(to, frm):
        return remote(codes.at[d, frm], codes.at[d, frm], code_s, code_r, {"mp": to})

    def plane_copy(to, frm):
        return remote(codes.at[frm], codes.at[frm], plane_s, plane_r, {"dp": to})

    def forward_q(k):
        if k:
            for h in (up(k), up(8 - k)):
                wait_batch(qall.at[h], q_r.at[h])
        for to, h, rows in ((right, up(8 - k) if k else z, pl.ds(0, 16)), (left, up(k), pl.ds(16, 16))):
            block = qall.at[h] if k < 3 else qall.at[h, rows]
            remote(block, block, q_s, q_r.at[h], {"mp": to}).start()

    def fetch_copy(pair, to, frm):
        return remote(fetch.at[pair, to], cands.at[pair, frm], fetch_s.at[pair], fetch_r.at[pair], {"dp": to})

    def piece_copy(to, frm):
        return remote(pieces.at[to // 2], pieces_in.at[frm], piece_s, piece_r, {"mp": to})

    def index_copy(to, frm):
        return remote(slots.at[to], index_ref.at[frm], idx_s, idx_r, owner(to))

    def sums_copy(to, frm):
        return remote(sums.at[to], sums_in.at[frm], sums_s, sums_r, {"mp": to})

    def draw_copy(to, frm):
        return remote(draw.at[lax.rem(to, 2)], draws.at[frm], draw_s, draw_r, {"mp": to})

    def grad_copy(to, frm):
        return remote(gshare.at[to], gshare_in.at[frm], grad_s, grad_r, owner(to))

    def wait_batch(ref, semaphore):
        pltpu.make_async_copy(ref, ref, semaphore).wait()

    def spot(way, u):
        if u == 0:
            dist, half = 4, way
        elif u % 2 == 1:
            dist, half = 4 - (u + 1) // 2, 1 - way
        else:
            dist, half = 4 - u // 2, way
        return part_of(way, dist), half

    def c_copy(way, n):
        i, half = spot(way, n // 2)
        start = half * 128 + n % 2 * 64
        return remote(
            cpart.at[i, start:start + 64], crecv.at[way, n], c_s.at[way, n % 2], c_r.at[way, n],
            {"mp": right if way == 0 else left})

    def qp_copy(way, u):
        i, half = spot(way, u)
        return remote(
            qpart.at[i, half * 16:half * 16 + 16], qrecv.at[way, u], qp_s.at[way, u % 2], qp_r.at[way, u],
            {"mp": right if way == 0 else left})

    def q_unit(way, u):
        i, half = spot(way, u)
        rows = slice(half * 16, half * 16 + 16)
        if u >= 2:
            qp_copy(way, u - 2).wait_recv()
            qpart[i, rows] = (qpart[i, rows].astype(f32) + qrecv[way, u - 2].astype(f32)).astype(bf16)
            qp_copy(way, u - 2).wait_send()
        qp_copy(way, u).start()

    def c_unit(way, n):
        i, half = spot(way, n // 2)
        rows = slice(half * 128 + n % 2 * 64, half * 128 + n % 2 * 64 + 64)
        if n >= 4:
            c_copy(way, n - 4).wait_recv()
            cpart[i, rows] = (cpart[i, rows].astype(f32) + crecv[way, n - 4].astype(f32)).astype(bf16)
        if n >= 2:
            c_copy(way, n - 2).wait_send()
        c_copy(way, n).start()

    def c_units(u):
        for n in (2 * u, 2 * u + 1):
            c_unit(0, n)
            c_unit(1, n)

    def both_units(u):
        q_unit(0, u)
        q_unit(1, u)
        c_units(u)

    def normalise(i, slot):
        for r in range(0, 256, 32):
            v = x[i, r:r + 32, :].astype(f32)
            scale = lax.rsqrt(jnp.mean(v * v, axis=-1, keepdims=True) + norm_eps)
            normed[slot, r:r + 32, :] = (v * scale * gain[...]).astype(bf16)

    def index_places():
        for load in load_small[1:]:
            load.wait()
        sub = lax.broadcasted_iota(jnp.int32, (256, 256), 0)
        lane = lax.broadcasted_iota(jnp.int32, (256, 256), 1)
        spread = jnp.where((lane[0:32] & 31) == sub[0:32], 1.0, 0.0).astype(bf16)
        of_row = (lane[0:8] >> 5) == sub[0:8]

        def flat(block):
            wide = jnp.dot(block.astype(f32).astype(bf16), spread, preferred_element_type=f32)
            return jnp.sum(jnp.where(of_row, wide, 0.0), axis=0, keepdims=True)

        def rank(row, earlier):
            column_form = jnp.sum(jnp.where(lane == sub, row, 0.0), axis=1, keepdims=True)
            return jnp.sum(jnp.where((column_form == row) & earlier, 1.0, 0.0), axis=0, keepdims=True)

        owners = flat(asked[...])
        slot = owners * 8.0 + rank(owners, (sub & 31) < (lane & 31))
        code = (slot * 256.0 + flat(row_of[...])).astype(jnp.int32)
        codes[d, z] = code
        goal = dest[...].astype(f32)
        idx[...] = (goal * 16.0 + rank(goal, sub < lane)).astype(jnp.int32)

    load_x(0).wait()
    load_small[0].wait()
    load_out.wait()
    load_proj.wait()
    normalise(0, 0)
    woutp[...] = jnp.dot(wout[...], proj[...], preferred_element_type=f32).astype(bf16)
    load_in.wait()

    @pl.loop(0, 9)
    def _(i):
        @pl.when(i == 0)
        def _():
            load_q.wait()

        @pl.when(jnp.logical_and(i > 0, i < 8))
        def _():
            load_x(i + 1).wait()

        slot = lax.rem(i, 2)
        for n in range(2):
            rows = normed[slot]
            gate = jnp.dot(rows, win[:, n * 256:(n + 1) * 256], preferred_element_type=f32)
            upper = jnp.dot(rows, win[:, 512 + n * 256:768 + n * 256], preferred_element_type=f32)
            hidden[:, n * 256:(n + 1) * 256] = (gate / (1.0 + jnp.exp(-gate)) * upper).astype(bf16)
        normalise(jnp.minimum(i + 1, 8), 1 - slot)

        @pl.when(i == 0)
        def _():
            pl.semaphore_wait(barrier, 38)

        @pl.when(i == 1)
        def _():
            normed[1] = jnp.dot(hidden[...], wout[...], preferred_element_type=f32).astype(bf16)
            for k in (0, 2, 3, 4, 5, 6, 7, 8):
                h = home_of(jnp.int32(k))
                qpart[k] = normed[1, pl.ds(pl.multiple_of(h * 32, 32), 32), :]
            q_unit(0, 0)
            q_unit(1, 0)
            index_places()

            @pl.loop(1, 8)
            def _(s):
                code_copy(up(s), z).start()

        @pl.when(i != 1)
        def _():
            cpart[i] = jnp.dot(hidden[...], woutp[...], preferred_element_type=f32).astype(bf16)

        @pl.when(i == 0)
        def _():
            c_units(0)

        @pl.when(i == 3)
        def _():
            both_units(1)

        @pl.when(i == 5)
        def _():
            both_units(2)

        @pl.when(i == 6)
        def _():
            wait_batch(codes.at[d, 0:7], code_r)

            @pl.loop(1, 16)
            def _(s):
                plane_copy(lax.rem(d + s, 16), d).start()

        @pl.when(i == 7)
        def _():
            both_units(3)

    base[...] = jnp.dot(x[8], proj[...], preferred_element_type=f32) + cpart[8].astype(f32)
    both_units(4)
    wait_batch(codes.at[0:15], plane_r)

    owner_slot = (d * 8 + z) * 8

    def wanted(pair):
        rank = lax.broadcasted_iota(jnp.int32, (8, 256), 0)
        lane = lax.broadcasted_iota(jnp.int32, (8, 256), 1)
        for c in range(16):
            for k in range(2):
                code = codes[c, pair * 2 + k]
                hit = (code >> 8) == owner_slot + rank
                row = jnp.sum(jnp.where(hit, (code & 255) + 1, 0), axis=1, keepdims=True) - 1
                packed[c * 16 + k * 8:c * 16 + k * 8 + 8, :] = jnp.where(lane == row, 1.0, 0.0)
        onehots[pair] = packed[...].astype(bf16)

    @pl.loop(0, 4)
    def _(pair):
        wanted(pair)

    both_units(5)

    @pl.loop(0, 8)
    def _(m):
        sub = lax.broadcasted_iota(jnp.int32, (32, 256), 0)
        lane = lax.broadcasted_iota(jnp.int32, (32, 256), 1)
        code = codes[d, m]
        wants = jnp.zeros((32, 128), jnp.int32)
        for k in range(8):
            of_k = jnp.sum(jnp.where(lane - k * 32 == sub, code, 0), axis=1, keepdims=True)
            wants = jnp.where(lane[:, 0:128] == k, of_k, wants)
        column[m] = wants

    both_units(6)

    for way in (0, 1):
        for u in (5, 6):
            qp_copy(way, u).wait_recv()
    for half in range(2):
        rows = slice(half * 16, half * 16 + 16)
        own = x[1, pl.ds(pl.multiple_of(z * 32 + half * 16, 16), 16), :].astype(f32)
        mixed = (
            qpart[8, rows].astype(f32) + qrecv[0, 6 - half].astype(f32) + qrecv[1, 5 + half].astype(f32))
        sumq[rows, :] = (own + mixed).astype(bf16)
    raw = jnp.dot(sumq[...], proj[...], preferred_element_type=f32)
    length = jnp.sqrt(jnp.sum(raw * raw, axis=-1, keepdims=True) + embed_eps)
    unit = raw / length
    embq[...] = unit.astype(bf16)
    qall[z] = embq[...]
    forward_q(0)

    for r in range(2):
        for way in (0, 1):
            c_copy(way, 10 + r).wait_recv()
            c_copy(way, 12 + r).wait_recv()
        for half in range(2):
            rows = slice(half * 128 + r * 64, half * 128 + r * 64 + 64)
            raw_c = (
                base[rows, :] + crecv[0, 12 - 2 * half + r].astype(f32) + crecv[1, 10 + 2 * half + r].astype(f32))
            inverse = lax.rsqrt(jnp.sum(raw_c * raw_c, axis=-1, keepdims=True) + embed_eps)
            embc[rows, :] = (raw_c * inverse).astype(bf16)

    def pair_at(s):
        return lax.rem(z // 2 + 1 + s, 4)

    def send_fetch(s):
        pair = pair_at(s)
        for dy, dx in FAR_FIRST:
            fetch_copy(pair, across(dy, dx), d).start()

    @pl.loop(0, 4)
    def _(s):
        pair = pair_at(s)
        rows = jnp.dot(onehots[pair], embc[...], preferred_element_type=f32).astype(bf16)
        fetch[pair] = rows.reshape(16, 16, 768)

        @pl.when(s == 0)
        def _():
            send_fetch(0)

        cands[pair, d] = fetch[pair, d]

    forward_q(1)

    turned = sumq[...].astype(f32).T.reshape(32, 4, 8, 32)
    for k in range(4):
        pieces[k] = turned[:, k].reshape(256, 32).T.astype(bf16)

    @pl.loop(1, 8)
    def _(s):
        piece_copy(up(s), z).start()

    pieces_in[z] = pieces[z // 2]
    send_fetch(1)
    forward_q(2)

    @pl.loop(0, 2)
    def _(s):
        row = lax.broadcasted_iota(jnp.int32, (256, 256), 0) + s * 256
        onehot = jnp.where(row == idx[...], 1.0, 0.0).astype(bf16)
        rows = jnp.dot(onehot, embc[...], preferred_element_type=f32).astype(bf16)
        slots[pl.ds(s * 16, 16)] = rows.reshape(16, 16, 768)

    diagonal = lax.broadcasted_iota(jnp.int32, (32, 32), 0) == lax.broadcasted_iota(jnp.int32, (32, 32), 1)
    pos_column = jnp.sum(jnp.where(diagonal, pos[...], 0), axis=1, keepdims=True)
    at_pos = lax.broadcasted_iota(jnp.int32, (32, 256), 1) == pos_column
    positive = jnp.dot(jnp.where(at_pos, 1.0, 0.0).astype(bf16), embc[...], preferred_element_type=f32)
    pos_score = score_scale * jnp.sum(embq[...].astype(f32) * positive, axis=1, keepdims=True)
    pos_weight = jnp.exp(pos_score)

    forward_q(3)

    @pl.loop(0, 4)
    def _(s):
        pair = pair_at(s)
        wait_batch(cands.at[pair, 0:15], fetch_r.at[pair])
        wait_batch(fetch.at[pair, 0:15], fetch_s.at[pair])

        @pl.when(s < 2)
        def _():
            send_fetch(s + 2)

        @pl.when(s == 1)
        def _():
            wait_batch(qall.at[up(4)], q_r.at[up(4)])

        q = qall[pl.ds(pair * 2, 2)].reshape(64, 768)
        cand = cands[pair].reshape(256, 768)
        score = score_scale * lax.dot_general(
            q, cand, (((1,), (1,)), ((), ())), preferred_element_type=f32)
        row = lax.broadcasted_iota(jnp.int32, (64, 256), 0)
        lane = lax.broadcasted_iota(jnp.int32, (64, 256), 1)
        slot = ((lane >> 4) * 8 + z) * 8 + (lane & 7)
        wants = column[pl.ds(pair * 2, 2)].reshape(64, 128)
        hit = (wants[:, 0:1] >> 8) == slot
        for k in range(1, 8):
            hit = hit | ((wants[:, k:k + 1] >> 8) == slot)
        hit = hit & ((row >> 5) == ((lane >> 3) & 1))
        weight = jnp.where(hit, jnp.exp(score), 0.0)
        total = jnp.sum(weight, axis=1, keepdims=True)
        summed = jnp.dot(weight.astype(bf16), cand, preferred_element_type=f32).astype(bf16)
        high = total.astype(bf16).astype(f32)
        first = lax.broadcasted_iota(jnp.int32, (64, 128), 1) < 64
        tail = jnp.where(first, high, total - high).astype(bf16)
        for k in range(2):
            sums[pair * 2 + k, :, 0:768] = summed[k * 32:(k + 1) * 32]
            sums[pair * 2 + k, :, 768:896] = tail[k * 32:(k + 1) * 32]

            @pl.when(pair * 2 + k != z)
            def _():
                sums_copy(pair * 2 + k, z).start()

    sums_in[z] = sums[z]
    own_index = pltpu.make_async_copy(slots.at[here], index_ref.at[here], own_s)
    own_index.start()
    for dy, dx in FAR_FIRST:
        for k in range(2):
            index_copy(k * 16 + across(dy, dx), here).start()
    index_copy((1 - g) * 16 + d, here).start()

    wait_batch(pieces_in.at[0:7], piece_r)
    turned_in[...] = pieces_in[...].reshape(256, 256).astype(f32).T.astype(bf16)
    wait_batch(sums_in.at[0:7], sums_r)

    gathered = sums_in[0].astype(f32)
    for m in range(1, 8):
        gathered = gathered + sums_in[m].astype(f32)
    total = gathered[:, 768:769] + gathered[:, 832:833] + pos_weight
    loss = jnp.log(total) - pos_score
    loss_ref[...] = jnp.sum(jnp.where(diagonal, loss, 0.0), axis=0, keepdims=True)
    dunit = score_scale * ((gathered[:, 0:768] + pos_weight * positive) / total - positive)
    along = jnp.sum(unit * dunit, axis=1, keepdims=True)
    drawn = ((dunit - unit * along) / length).astype(bf16)
    draw[0] = drawn[:, 0:384]
    draw[1] = drawn[:, 384:768]
    for s in (4, 3, 5, 2, 6, 1, 7):
        draw_copy(up(s), z).start()
    parity = lax.rem(z, 2)
    draws[z] = draw[parity]
    wait_batch(draws.at[0:7], draw_r)
    gshare[...] = jnp.dot(
        turned_in[...], draws[...].reshape(256, 384), preferred_element_type=f32).reshape(32, 8, 384)
    for dy, dx in FAR_FIRST:
        for k in range(2):
            grad_copy(k * 16 + across(dy, dx), here).start()
    grad_copy((1 - g) * 16 + d, here).start()
    gshare_in[here] = gshare[here]

    for way in (0, 1):
        for u in (5, 6):
            qp_copy(way, u).wait_send()
        for n in (12, 13):
            c_copy(way, n).wait_send()
    wait_batch(codes.at[d, 0:7], code_s)
    wait_batch(codes.at[0:15], plane_s)
    wait_batch(qall.at[0:7], q_s)
    wait_batch(pieces_in.at[0:7], piece_s)
    wait_batch(sums.at[0:7], sums_s)
    wait_batch(draws.at[0:7], draw_s)
    own_index.wait()
    wait_batch(slots.at[0:31], idx_s)
    wait_batch(index_ref.at[0:31], idx_r)
    wait_batch(gshare_in.at[0:31], grad_r)
    gpart[parity] = jnp.sum(gshare_in[...], axis=0)
    swap = remote(gpart.at[parity], gpart.at[parity], part_s, part_r, {"mp": z + 1 - 2 * parity})
    swap.start()
    wait_batch(gshare.at[0:31], grad_s)
    wait_batch(gpart.at[0], part_r)
    for k in range(2):
        grad_ref[:, k * 384:(k + 1) * 384] = jnp.where(parity == 0, gpart[k, 0:4], gpart[k, 4:8])
    swap.wait_send()


def fused(*args):
    hbm = pl.BlockSpec(memory_space=pl.ANY)
    vmem = pl.BlockSpec(memory_space=pltpu.VMEM)
    sds = jax.ShapeDtypeStruct
    dma = pltpu.SemaphoreType.DMA
    return pl.pallas_call(
        kernel,
        out_shape=(sds((1, 32), f32), sds((4, 768), f32), sds((32, 16, 768), bf16)),
        in_specs=[hbm] * 10,
        out_specs=[vmem, vmem, hbm],
        scratch_shapes=[
            pltpu.VMEM((9, 256, 1024), bf16),
            pltpu.VMEM((1024, 1024), bf16),
            pltpu.VMEM((512, 1024), bf16),
            pltpu.VMEM((1024, 768), bf16),
            pltpu.VMEM((512, 768), bf16),
            pltpu.VMEM((2, 256, 1024), bf16),
            pltpu.VMEM((256, 512), bf16),
            pltpu.VMEM((9, 256, 768), bf16),
            pltpu.VMEM((9, 32, 1024), bf16),
            pltpu.VMEM((256, 768), f32),
            pltpu.VMEM((2, 14, 64, 768), bf16),
            pltpu.VMEM((2, 7, 16, 1024), bf16),
            pltpu.VMEM((1, 1024), f32),
            pltpu.VMEM((1, 32), jnp.int32),
            pltpu.VMEM((8, 32), jnp.int32),
            pltpu.VMEM((8, 32), jnp.int32),
            pltpu.VMEM((1, 256), jnp.int32),
            pltpu.VMEM((1, 256), jnp.int32),
            pltpu.VMEM((16, 8, 1, 256), jnp.int32),
            pltpu.VMEM((8, 32, 128), jnp.int32),
            pltpu.VMEM((4, 256, 256), bf16),
            pltpu.VMEM((256, 256), f32),
            pltpu.VMEM((256, 768), bf16),
            pltpu.VMEM((32, 768), bf16),
            pltpu.VMEM((32, 1024), bf16),
            pltpu.VMEM((4, 16, 16, 768), bf16),
            pltpu.VMEM((4, 16, 16, 768), bf16),
            pltpu.VMEM((8, 32, 768), bf16),
            pltpu.VMEM((32, 16, 768), bf16),
            pltpu.VMEM((4, 32, 256), bf16),
            pltpu.VMEM((8, 32, 256), bf16),
            pltpu.VMEM((256, 256), bf16),
            pltpu.VMEM((8, 32, 896), bf16),
            pltpu.VMEM((8, 32, 896), bf16),
            pltpu.VMEM((2, 32, 384), bf16),
            pltpu.VMEM((8, 32, 384), bf16),
            pltpu.VMEM((32, 8, 384), f32),
            pltpu.VMEM((32, 8, 384), f32),
            pltpu.VMEM((2, 8, 384), f32),
            dma((17,)), dma((2, 2)), dma((2, 14)), dma((2, 2)), dma((2, 7)), dma((8,)), dma((4,)), dma((4,)),
            *[dma] * 18,
        ],
        compiler_params=pltpu.CompilerParams(
            collective_id=0, has_side_effects=True, vmem_limit_bytes=52 * 1024 * 1024),
        cost_estimate=pl.CostEstimate(flops=11_000_000_000, bytes_accessed=20_000_000, transcendentals=2_000_000),
        name="fused",
    )(*args)


def per_device(
    queries, clips, norm_gain, w_in, w_out, proj, pos_row, neg_owner, neg_row, clip_dest
):
    width = queries.shape[1]
    loss, grad, index = fused(
        queries, clips, norm_gain.reshape(1, width), w_in.reshape(width, -1), w_out, proj,
        pos_row.reshape(1, -1), neg_owner.T, neg_row.T, clip_dest.reshape(1, -1))
    return (loss.reshape(-1), index.reshape(-1, index.shape[-1]), grad)


def solution(mesh):
    return jax.shard_map(
        per_device,
        mesh=mesh,
        in_specs=(
            P(("group", "dp"), None),
            P(("group", "dp"), None),
            P(),
            P(None, None, "mp"),
            P("mp", None),
            P(),
            P(("group", "dp", "mp")),
            P(("group", "dp", "mp"), None),
            P(("group", "dp", "mp"), None),
            P(("group", "dp", "mp"), None),
        ),
        out_specs=(
            P(("group", "dp", "mp")),
            P(("group", "dp", "mp"), None),
            P(("group", "dp", "mp"), None),
        ),
        check_vma=False,
    )
```

```python
import jax
import jax.numpy as jnp
from jax import lax
from jax.experimental import pallas as pl
from jax.experimental.pallas import tpu as pltpu
from jax.sharding import PartitionSpec as P

norm_eps = 1e-06
embed_eps = 1e-06
score_scale = 20.0
MESH = pl.DeviceIdType.MESH
f32 = jnp.float32
bf16 = jnp.bfloat16
FAR_FIRST = (
    (2, 2), (3, 2), (2, 3), (2, 1), (1, 2), (3, 1), (1, 3), (3, 3), (1, 1), (0, 2), (2, 0), (3, 0), (0, 3), (1, 0),
    (0, 1),
)


def part_of(way, dist):
    return 0 if dist == 4 else 8 - 2 * dist + way


def kernel(
    q_hbm, c_hbm, gain_hbm, win_hbm, wout_hbm, proj_hbm, pos_hbm, asked_hbm, row_hbm, dest_hbm,
    loss_ref, grad_ref, index_ref,
    x, win, wout, proj, woutp, normed, hidden, cpart, qpart, base, crecv, qrecv,
    gain, pos, asked, row_of, dest, idx, codes, column, onehots, packed, embc, embq, sumq,
    fetch, cands, qall, slots, pieces, pieces_in, turned_in, sums, sums_in, draw, draws, gshare, gshare_in, gpart,
    load_sem, c_s, c_r, qp_s, qp_r, q_r, fetch_s, fetch_r,
    code_s, code_r, plane_s, plane_r, q_s, piece_s, piece_r, own_s, idx_s, idx_r, sums_s, sums_r, draw_s, draw_r,
    grad_s, grad_r, part_s, part_r,
):
    g, d, z = lax.axis_index("group"), lax.axis_index("dp"), lax.axis_index("mp")
    y, xx = d // 4, lax.rem(d, 4)
    here = g * 16 + d
    right, left = lax.rem(z + 1, 8), lax.rem(z + 7, 8)

    def up(s):
        return lax.rem(z + s, 8)

    def across(dy, dx):
        return lax.rem(y + dy, 4) * 4 + lax.rem(xx + dx, 4)

    def owner(o):
        return {"group": o // 16, "dp": lax.rem(o, 16)}

    def remote(src, dst, send, recv, target):
        return pltpu.make_async_remote_copy(
            src_ref=src, dst_ref=dst, send_sem=send, recv_sem=recv, device_id=target, device_id_type=MESH)

    def home_of(i):
        even = (8 - i) // 2
        odd = 8 - (9 - i) // 2
        return lax.rem(z + jnp.where(lax.rem(i, 2) == 0, even, odd), 8)

    def load_x(i):
        rows = pl.ds(pl.multiple_of(home_of(jnp.int32(i)) * 256, 256), 256)
        return pltpu.make_async_copy(c_hbm.at[rows], x.at[i], load_sem.at[i])

    load_q = pltpu.make_async_copy(q_hbm, x.at[1], load_sem.at[1])
    load_in = pltpu.make_async_copy(win_hbm, win, load_sem.at[9])
    load_out = pltpu.make_async_copy(wout_hbm, wout, load_sem.at[10])
    load_proj = pltpu.make_async_copy(proj_hbm, proj, load_sem.at[11])
    load_small = [
        pltpu.make_async_copy(src, dst, load_sem.at[12 + k])
        for k, (src, dst) in enumerate((
            (gain_hbm, gain), (asked_hbm, asked), (row_hbm, row_of), (dest_hbm, dest), (pos_hbm, pos)))
    ]
    load_x(0).start()
    load_small[0].start()
    load_out.start()
    load_proj.start()
    load_in.start()
    load_q.start()
    for i in range(2, 9):
        load_x(i).start()

    for load in load_small[1:]:
        load.start()

    barrier = pltpu.get_barrier_semaphore()

    @pl.loop(1, 32)
    def _(s):
        pl.semaphore_signal(barrier, inc=1, device_id=owner(lax.rem(here + s, 32)), device_id_type=MESH)

    @pl.loop(1, 8)
    def _(s):
        pl.semaphore_signal(barrier, inc=1, device_id={"mp": up(s)}, device_id_type=MESH)

    def code_copy(to, frm):
        return remote(codes.at[d, frm], codes.at[d, frm], code_s, code_r, {"mp": to})

    def plane_copy(to, frm):
        return remote(codes.at[frm], codes.at[frm], plane_s, plane_r, {"dp": to})

    def send_q(h, to, rows=None):
        block = qall.at[h] if rows is None else qall.at[h, rows]
        remote(block, block, q_s, q_r.at[h], {"mp": to}).start()

    def wait_q(h):
        wait_batch(qall.at[h], q_r.at[h])

    def fetch_copy(pair, to, frm):
        return remote(fetch.at[pair, to], cands.at[pair, frm], fetch_s.at[pair], fetch_r.at[pair], {"dp": to})

    def piece_copy(to, frm):
        return remote(pieces.at[to // 2], pieces_in.at[frm], piece_s, piece_r, {"mp": to})

    def index_copy(to, frm):
        return remote(slots.at[to], index_ref.at[frm], idx_s, idx_r, owner(to))

    def sums_copy(to, frm):
        return remote(sums.at[to], sums_in.at[frm], sums_s, sums_r, {"mp": to})

    def draw_copy(to, frm):
        return remote(draw.at[lax.rem(to, 2)], draws.at[frm], draw_s, draw_r, {"mp": to})

    def grad_copy(to, frm):
        return remote(gshare.at[to], gshare_in.at[frm], grad_s, grad_r, owner(to))

    def wait_batch(ref, semaphore):
        pltpu.make_async_copy(ref, ref, semaphore).wait()

    def spot(way, u):
        if u == 0:
            dist, half = 4, way
        elif u % 2 == 1:
            dist, half = 4 - (u + 1) // 2, 1 - way
        else:
            dist, half = 4 - u // 2, way
        return part_of(way, dist), half

    def c_copy(way, n):
        i, half = spot(way, n // 2)
        start = half * 128 + n % 2 * 64
        return remote(
            cpart.at[i, start:start + 64], crecv.at[way, n], c_s.at[way, n % 2], c_r.at[way, n],
            {"mp": right if way == 0 else left})

    def qp_copy(way, u):
        i, half = spot(way, u)
        return remote(
            qpart.at[i, half * 16:half * 16 + 16], qrecv.at[way, u], qp_s.at[way, u % 2], qp_r.at[way, u],
            {"mp": right if way == 0 else left})

    def q_unit(way, u):
        i, half = spot(way, u)
        rows = slice(half * 16, half * 16 + 16)
        if u >= 2:
            qp_copy(way, u - 2).wait_recv()
            qpart[i, rows] = (qpart[i, rows].astype(f32) + qrecv[way, u - 2].astype(f32)).astype(bf16)
            qp_copy(way, u - 2).wait_send()
        qp_copy(way, u).start()

    def c_unit(way, n):
        i, half = spot(way, n // 2)
        rows = slice(half * 128 + n % 2 * 64, half * 128 + n % 2 * 64 + 64)
        if n >= 4:
            c_copy(way, n - 4).wait_recv()
            cpart[i, rows] = (cpart[i, rows].astype(f32) + crecv[way, n - 4].astype(f32)).astype(bf16)
        if n >= 2:
            c_copy(way, n - 2).wait_send()
        c_copy(way, n).start()

    def c_units(u):
        for n in (2 * u, 2 * u + 1):
            c_unit(0, n)
            c_unit(1, n)

    def both_units(u):
        q_unit(0, u)
        q_unit(1, u)
        c_units(u)

    def normalise(i, slot):
        for r in range(0, 256, 32):
            v = x[i, r:r + 32, :].astype(f32)
            scale = lax.rsqrt(jnp.mean(v * v, axis=-1, keepdims=True) + norm_eps)
            normed[slot, r:r + 32, :] = (v * scale * gain[...]).astype(bf16)

    def index_places():
        for load in load_small[1:]:
            load.wait()
        sub = lax.broadcasted_iota(jnp.int32, (256, 256), 0)
        lane = lax.broadcasted_iota(jnp.int32, (256, 256), 1)
        spread = jnp.where((lane[0:32] & 31) == sub[0:32], 1.0, 0.0).astype(bf16)
        of_row = (lane[0:8] >> 5) == sub[0:8]

        def flat(block):
            wide = jnp.dot(block.astype(f32).astype(bf16), spread, preferred_element_type=f32)
            return jnp.sum(jnp.where(of_row, wide, 0.0), axis=0, keepdims=True)

        def rank(row, earlier):
            column_form = jnp.sum(jnp.where(lane == sub, row, 0.0), axis=1, keepdims=True)
            return jnp.sum(jnp.where((column_form == row) & earlier, 1.0, 0.0), axis=0, keepdims=True)

        owners = flat(asked[...])
        slot = owners * 8.0 + rank(owners, (sub & 31) < (lane & 31))
        code = (slot * 256.0 + flat(row_of[...])).astype(jnp.int32)
        codes[d, z] = code
        goal = dest[...].astype(f32)
        idx[...] = (goal * 16.0 + rank(goal, sub < lane)).astype(jnp.int32)

    load_x(0).wait()
    load_small[0].wait()
    load_out.wait()
    load_proj.wait()
    normalise(0, 0)
    woutp[...] = jnp.dot(wout[...], proj[...], preferred_element_type=f32).astype(bf16)
    load_in.wait()

    @pl.loop(0, 9)
    def _(i):
        @pl.when(i == 0)
        def _():
            load_q.wait()

        @pl.when(jnp.logical_and(i > 0, i < 8))
        def _():
            load_x(i + 1).wait()

        slot = lax.rem(i, 2)
        for n in range(2):
            rows = normed[slot]
            gate = jnp.dot(rows, win[0, :, n * 256:(n + 1) * 256], preferred_element_type=f32)
            upper = jnp.dot(rows, win[1, :, n * 256:(n + 1) * 256], preferred_element_type=f32)
            hidden[:, n * 256:(n + 1) * 256] = (gate / (1.0 + jnp.exp(-gate)) * upper).astype(bf16)
        normalise(jnp.minimum(i + 1, 8), 1 - slot)

        @pl.when(i == 0)
        def _():
            pl.semaphore_wait(barrier, 38)

        @pl.when(i == 1)
        def _():
            normed[1] = jnp.dot(hidden[...], wout[...], preferred_element_type=f32).astype(bf16)
            for k in (0, 2, 3, 4, 5, 6, 7, 8):
                h = home_of(jnp.int32(k))
                qpart[k] = normed[1, pl.ds(pl.multiple_of(h * 32, 32), 32), :]
            q_unit(0, 0)
            q_unit(1, 0)
            index_places()

            @pl.loop(1, 8)
            def _(s):
                code_copy(up(s), z).start()

        @pl.when(i != 1)
        def _():
            cpart[i] = jnp.dot(hidden[...], woutp[...], preferred_element_type=f32).astype(bf16)

        @pl.when(i == 0)
        def _():
            c_units(0)

        @pl.when(i == 3)
        def _():
            both_units(1)

        @pl.when(i == 5)
        def _():
            both_units(2)

        @pl.when(i == 6)
        def _():
            wait_batch(codes.at[d, 0:7], code_r)

            @pl.loop(1, 16)
            def _(s):
                plane_copy(lax.rem(d + s, 16), d).start()

        @pl.when(i == 7)
        def _():
            both_units(3)

    base[...] = jnp.dot(x[8], proj[...], preferred_element_type=f32) + cpart[8].astype(f32)
    both_units(4)
    wait_batch(codes.at[0:15], plane_r)

    owner_slot = (d * 8 + z) * 8

    def wanted(pair):
        rank = lax.broadcasted_iota(jnp.int32, (8, 256), 0)
        lane = lax.broadcasted_iota(jnp.int32, (8, 256), 1)
        for c in range(16):
            for k in range(2):
                code = codes[c, pair * 2 + k]
                hit = (code >> 8) == owner_slot + rank
                row = jnp.sum(jnp.where(hit, (code & 255) + 1, 0), axis=1, keepdims=True) - 1
                packed[c * 16 + k * 8:c * 16 + k * 8 + 8, :] = jnp.where(lane == row, 1.0, 0.0)
        onehots[pair] = packed[...].astype(bf16)

    @pl.loop(0, 4)
    def _(pair):
        wanted(pair)

    both_units(5)

    @pl.loop(0, 8)
    def _(m):
        sub = lax.broadcasted_iota(jnp.int32, (32, 256), 0)
        lane = lax.broadcasted_iota(jnp.int32, (32, 256), 1)
        code = codes[d, m]
        wants = jnp.zeros((32, 128), jnp.int32)
        for k in range(8):
            of_k = jnp.sum(jnp.where(lane - k * 32 == sub, code, 0), axis=1, keepdims=True)
            wants = jnp.where(lane[:, 0:128] == k, of_k, wants)
        column[m] = wants

    both_units(6)

    for way in (0, 1):
        for u in (5, 6):
            qp_copy(way, u).wait_recv()
    for half in range(2):
        rows = slice(half * 16, half * 16 + 16)
        own = x[1, pl.ds(pl.multiple_of(z * 32 + half * 16, 16), 16), :].astype(f32)
        mixed = (
            qpart[8, rows].astype(f32) + qrecv[0, 6 - half].astype(f32) + qrecv[1, 5 + half].astype(f32))
        sumq[rows, :] = (own + mixed).astype(bf16)
    raw = jnp.dot(sumq[...], proj[...], preferred_element_type=f32)
    length = jnp.sqrt(jnp.sum(raw * raw, axis=-1, keepdims=True) + embed_eps)
    unit = raw / length
    embq[...] = unit.astype(bf16)
    qall[z] = embq[...]
    for s in (2, 6, 1, 7):
        send_q(z, up(s))

    for r in range(2):
        for way in (0, 1):
            c_copy(way, 10 + r).wait_recv()
            c_copy(way, 12 + r).wait_recv()
        for half in range(2):
            rows = slice(half * 128 + r * 64, half * 128 + r * 64 + 64)
            raw_c = (
                base[rows, :] + crecv[0, 12 - 2 * half + r].astype(f32) + crecv[1, 10 + 2 * half + r].astype(f32))
            inverse = lax.rsqrt(jnp.sum(raw_c * raw_c, axis=-1, keepdims=True) + embed_eps)
            embc[rows, :] = (raw_c * inverse).astype(bf16)

    def pair_at(s):
        return lax.rem(z // 2 + 1 + s, 4)

    def send_fetch(s):
        pair = pair_at(s)
        for dy, dx in FAR_FIRST:
            fetch_copy(pair, across(dy, dx), d).start()

    @pl.loop(0, 4)
    def _(s):
        pair = pair_at(s)
        rows = jnp.dot(onehots[pair], embc[...], preferred_element_type=f32).astype(bf16)
        fetch[pair] = rows.reshape(16, 16, 768)

        @pl.when(s == 0)
        def _():
            send_fetch(0)

        cands[pair, d] = fetch[pair, d]


    turned = sumq[...].astype(f32).T.reshape(32, 4, 8, 32)
    for k in range(4):
        pieces[k] = turned[:, k].reshape(256, 32).T.astype(bf16)

    @pl.loop(1, 8)
    def _(s):
        piece_copy(up(s), z).start()

    pieces_in[z] = pieces[z // 2]
    send_fetch(1)
    wait_q(up(6))
    send_q(up(6), up(1))
    send_q(up(6), up(2), pl.ds(0, 16))
    wait_q(up(2))
    send_q(up(2), up(7))
    send_q(up(2), up(6), pl.ds(16, 16))

    @pl.loop(0, 2)
    def _(s):
        row = lax.broadcasted_iota(jnp.int32, (256, 256), 0) + s * 256
        onehot = jnp.where(row == idx[...], 1.0, 0.0).astype(bf16)
        rows = jnp.dot(onehot, embc[...], preferred_element_type=f32).astype(bf16)
        slots[pl.ds(s * 16, 16)] = rows.reshape(16, 16, 768)

    diagonal = lax.broadcasted_iota(jnp.int32, (32, 32), 0) == lax.broadcasted_iota(jnp.int32, (32, 32), 1)
    pos_column = jnp.sum(jnp.where(diagonal, pos[...], 0), axis=1, keepdims=True)
    at_pos = lax.broadcasted_iota(jnp.int32, (32, 256), 1) == pos_column
    positive = jnp.dot(jnp.where(at_pos, 1.0, 0.0).astype(bf16), embc[...], preferred_element_type=f32)
    pos_score = score_scale * jnp.sum(embq[...].astype(f32) * positive, axis=1, keepdims=True)
    pos_weight = jnp.exp(pos_score)

    for s in (1, 7, 3, 5):
        wait_q(up(s))

    @pl.loop(0, 4)
    def _(s):
        pair = pair_at(s)
        row = lax.broadcasted_iota(jnp.int32, (64, 256), 0)
        lane = lax.broadcasted_iota(jnp.int32, (64, 256), 1)
        slot = ((lane >> 4) * 8 + z) * 8 + (lane & 7)
        wants = column[pl.ds(pair * 2, 2)].reshape(64, 128)
        hit = (wants[:, 0:1] >> 8) == slot
        for k in range(1, 8):
            hit = hit | ((wants[:, k:k + 1] >> 8) == slot)
        hit = hit & ((row >> 5) == ((lane >> 3) & 1))
        wait_batch(cands.at[pair, 0:15], fetch_r.at[pair])
        wait_batch(fetch.at[pair, 0:15], fetch_s.at[pair])

        @pl.when(s < 2)
        def _():
            send_fetch(s + 2)

        @pl.when(s == 1)
        def _():
            wait_q(up(4))

        q = qall[pl.ds(pair * 2, 2)].reshape(64, 768)
        cand = cands[pair].reshape(256, 768)
        score = score_scale * lax.dot_general(
            q, cand, (((1,), (1,)), ((), ())), preferred_element_type=f32)
        weight = jnp.where(hit, jnp.exp(score), 0.0)
        total = jnp.sum(weight, axis=1, keepdims=True)
        summed = jnp.dot(weight.astype(bf16), cand, preferred_element_type=f32).astype(bf16)
        high = total.astype(bf16).astype(f32)
        first = lax.broadcasted_iota(jnp.int32, (64, 128), 1) < 64
        tail = jnp.where(first, high, total - high).astype(bf16)
        for k in range(2):
            sums[pair * 2 + k, :, 0:768] = summed[k * 32:(k + 1) * 32]
            sums[pair * 2 + k, :, 768:896] = tail[k * 32:(k + 1) * 32]

            @pl.when(pair * 2 + k != z)
            def _():
                sums_copy(pair * 2 + k, z).start()

    sums_in[z] = sums[z]
    own_index = pltpu.make_async_copy(slots.at[here], index_ref.at[here], own_s)
    own_index.start()
    for dy, dx in FAR_FIRST:
        for k in range(2):
            index_copy(k * 16 + across(dy, dx), here).start()
    index_copy((1 - g) * 16 + d, here).start()

    wait_batch(pieces_in.at[0:7], piece_r)
    turned_in[...] = pieces_in[...].reshape(256, 256).astype(f32).T.astype(bf16)
    wait_batch(sums_in.at[0:7], sums_r)

    gathered = sums_in[0].astype(f32)
    for m in range(1, 8):
        gathered = gathered + sums_in[m].astype(f32)
    total = gathered[:, 768:769] + gathered[:, 832:833] + pos_weight
    loss = jnp.log(total) - pos_score
    loss_ref[...] = jnp.sum(jnp.where(diagonal, loss, 0.0), axis=0, keepdims=True)
    dunit = score_scale * ((gathered[:, 0:768] + pos_weight * positive) / total - positive)
    along = jnp.sum(unit * dunit, axis=1, keepdims=True)
    drawn = ((dunit - unit * along) / length).astype(bf16)
    draw[0] = drawn[:, 0:384]
    draw[1] = drawn[:, 384:768]
    for s in (4, 3, 5, 2, 6, 1, 7):
        draw_copy(up(s), z).start()
    parity = lax.rem(z, 2)
    draws[z] = draw[parity]
    wait_batch(draws.at[0:7], draw_r)
    gshare[...] = jnp.dot(
        turned_in[...], draws[...].reshape(256, 384), preferred_element_type=f32).reshape(32, 8, 384)
    for dy, dx in FAR_FIRST:
        for k in range(2):
            grad_copy(k * 16 + across(dy, dx), here).start()
    grad_copy((1 - g) * 16 + d, here).start()
    gshare_in[here] = gshare[here]

    for way in (0, 1):
        for u in (5, 6):
            qp_copy(way, u).wait_send()
        for n in (12, 13):
            c_copy(way, n).wait_send()
    wait_batch(codes.at[d, 0:7], code_s)
    wait_batch(codes.at[0:15], plane_s)
    wait_batch(qall.at[0:7], q_s)
    wait_batch(pieces_in.at[0:7], piece_s)
    wait_batch(sums.at[0:7], sums_s)
    wait_batch(draws.at[0:7], draw_s)
    own_index.wait()
    wait_batch(slots.at[0:31], idx_s)
    wait_batch(index_ref.at[0:31], idx_r)
    wait_batch(gshare_in.at[0:31], grad_r)
    gpart[parity] = jnp.sum(gshare_in[...], axis=0)
    swap = remote(gpart.at[parity], gpart.at[parity], part_s, part_r, {"mp": z + 1 - 2 * parity})
    swap.start()
    wait_batch(gshare.at[0:31], grad_s)
    wait_batch(gpart.at[0], part_r)
    for k in range(2):
        grad_ref[:, k * 384:(k + 1) * 384] = jnp.where(parity == 0, gpart[k, 0:4], gpart[k, 4:8])
    swap.wait_send()


def fused(*args):
    hbm = pl.BlockSpec(memory_space=pl.ANY)
    vmem = pl.BlockSpec(memory_space=pltpu.VMEM)
    sds = jax.ShapeDtypeStruct
    dma = pltpu.SemaphoreType.DMA
    return pl.pallas_call(
        kernel,
        out_shape=(sds((1, 32), f32), sds((4, 768), f32), sds((32, 16, 768), bf16)),
        in_specs=[hbm] * 10,
        out_specs=[vmem, vmem, hbm],
        scratch_shapes=[
            pltpu.VMEM((9, 256, 1024), bf16),
            pltpu.VMEM((2, 1024, 512), bf16),
            pltpu.VMEM((512, 1024), bf16),
            pltpu.VMEM((1024, 768), bf16),
            pltpu.VMEM((512, 768), bf16),
            pltpu.VMEM((2, 256, 1024), bf16),
            pltpu.VMEM((256, 512), bf16),
            pltpu.VMEM((9, 256, 768), bf16),
            pltpu.VMEM((9, 32, 1024), bf16),
            pltpu.VMEM((256, 768), f32),
            pltpu.VMEM((2, 14, 64, 768), bf16),
            pltpu.VMEM((2, 7, 16, 1024), bf16),
            pltpu.VMEM((1, 1024), f32),
            pltpu.VMEM((1, 32), jnp.int32),
            pltpu.VMEM((8, 32), jnp.int32),
            pltpu.VMEM((8, 32), jnp.int32),
            pltpu.VMEM((1, 256), jnp.int32),
            pltpu.VMEM((1, 256), jnp.int32),
            pltpu.VMEM((16, 8, 1, 256), jnp.int32),
            pltpu.VMEM((8, 32, 128), jnp.int32),
            pltpu.VMEM((4, 256, 256), bf16),
            pltpu.VMEM((256, 256), f32),
            pltpu.VMEM((256, 768), bf16),
            pltpu.VMEM((32, 768), bf16),
            pltpu.VMEM((32, 1024), bf16),
            pltpu.VMEM((4, 16, 16, 768), bf16),
            pltpu.VMEM((4, 16, 16, 768), bf16),
            pltpu.VMEM((8, 32, 768), bf16),
            pltpu.VMEM((32, 16, 768), bf16),
            pltpu.VMEM((4, 32, 256), bf16),
            pltpu.VMEM((8, 32, 256), bf16),
            pltpu.VMEM((256, 256), bf16),
            pltpu.VMEM((8, 32, 896), bf16),
            pltpu.VMEM((8, 32, 896), bf16),
            pltpu.VMEM((2, 32, 384), bf16),
            pltpu.VMEM((8, 32, 384), bf16),
            pltpu.VMEM((32, 8, 384), f32),
            pltpu.VMEM((32, 8, 384), f32),
            pltpu.VMEM((2, 8, 384), f32),
            dma((17,)), dma((2, 2)), dma((2, 14)), dma((2, 2)), dma((2, 7)), dma((8,)), dma((4,)), dma((4,)),
            *[dma] * 18,
        ],
        compiler_params=pltpu.CompilerParams(
            collective_id=0, has_side_effects=True, vmem_limit_bytes=52 * 1024 * 1024),
        cost_estimate=pl.CostEstimate(flops=11_000_000_000, bytes_accessed=20_000_000, transcendentals=2_000_000),
        name="fused",
    )(*args)


def per_device(
    queries, clips, norm_gain, w_in, w_out, proj, pos_row, neg_owner, neg_row, clip_dest
):
    width = queries.shape[1]
    loss, grad, index = fused(
        queries, clips, norm_gain.reshape(1, width), w_in.transpose(1, 0, 2), w_out, proj,
        pos_row.reshape(1, -1), neg_owner.T, neg_row.T, clip_dest.reshape(1, -1))
    return (loss.reshape(-1), index.reshape(-1, index.shape[-1]), grad)


def solution(mesh):
    return jax.shard_map(
        per_device,
        mesh=mesh,
        in_specs=(
            P(("group", "dp"), None),
            P(("group", "dp"), None),
            P(),
            P(None, None, "mp"),
            P("mp", None),
            P(),
            P(("group", "dp", "mp")),
            P(("group", "dp", "mp"), None),
            P(("group", "dp", "mp"), None),
            P(("group", "dp", "mp"), None),
        ),
        out_specs=(
            P(("group", "dp", "mp")),
            P(("group", "dp", "mp"), None),
            P(("group", "dp", "mp"), None),
        ),
        check_vma=False,
    )
```
